256 devices in a mesh: blk: 32 (over z, x_hi, core), rep: 2 (over x_lo), feat: 4 (over y).
Axes of the slice: x: 4 (x_hi: 2, x_lo: 2; x = x_hi * 2 + x_lo), y: 4, z: 8, core: 2. Of those that a mesh axis runs over, the one named last changes fastest.
Arguments:
- features_t: bfloat16 [256, 16384], P('feat', 'blk'), may hold values from -6 to 6
- tile_values: bfloat16 [32, 32, 12, 128, 128], P('blk'), may hold values from 0 to 0.015319824
- tile_rows: int32 [32, 32, 12], P('blk'), may hold values from 0 to 3
- tile_cols: int32 [32, 32, 12], P('blk'), may hold values from 0 to 3
- tile_count: int32 [32, 32], P('blk'), may hold values from 1 to 12, as said below
- weight: bfloat16 [256, 256], P('feat'), may hold values from -0.375 to 0.375
- cotangent_t: bfloat16 [256, 16384], P('feat', 'blk'), may hold values from -6 to 6
Outputs:
- hidden_t: bfloat16 [256, 16384], P('feat', 'blk')
- weight_grad: float32 [256, 256], P('feat')
- input_grad_t: bfloat16 [256, 16384], P('feat', 'blk')
The draws below stay inside these ranges and needn't reach their ends.
Inputs may be any that keep to these rules, and one draw needn't show every extreme that they name: `tile_count`: section 0 (a partition's own tiles) always has 12 live slots; section k > 0 has between (c + 1) // 2 and c live slots, with c = max(1, 12 * (64 - k) // 64). `tile_rows`: several live tiles of a section may share a destination block or a source block.
All inputs are finite; a program needn't handle non-finite values.
Results may differ from the reference program's by a relative error of at most 0.027.
Values may be sent and summed in bfloat16 or wider, within the bound.
A program may use at most 128 MiB of HBM per device.

```python
import jax
import jax.numpy as jnp
from jax import lax

F = 256
H = 256
TILE = 128
BLOCKS = 4
TPS = 12
NODES = 16384
N_BLK = 32


def draw_tile_count(key, part):
    key = jax.random.fold_in(key, 11)
    section_ids = jnp.arange(N_BLK, dtype=jnp.int32)[None, :]
    ceiling = jnp.maximum(1, TPS * (2 * N_BLK - section_ids) // (2 * N_BLK))
    lowest = (ceiling + 1) // 2
    random_ints = jax.random.randint(key, (N_BLK, N_BLK), 0, 1 << 20)
    drawn = lowest + random_ints % (ceiling - lowest + 1)
    return jnp.where(section_ids == 0, TPS, drawn).astype(jnp.int32)


def set_ends(values, key, smallest, largest):
    index_at = [jax.random.randint(jax.random.fold_in(key, axis), (), 0, length) for axis, length in enumerate(values.shape)]
    longest = values.shape.index(max(values.shape))
    beside = index_at[:longest] + [(index_at[longest] + 1) % values.shape[longest]] + index_at[longest + 1:]
    return values.at[tuple(index_at)].set(smallest).at[tuple(beside)].set(largest)


def shard_levels(own_key, extent, split, least, largest):
    level = 1.0
    for axis_at, blocks in split:
        heights = jax.random.uniform(jax.random.fold_in(jax.random.fold_in(own_key, 6), axis_at), (blocks,), jnp.float32, least / len(split), largest / len(split))
        level = level * jnp.repeat(jnp.exp(heights), extent[axis_at] // blocks).reshape((-1,) + (1,) * (len(extent) - 1 - axis_at))
    return level


def scatter_about(key, extent, width, bound, pieces=(), held_as=jnp.bfloat16):
    result = width * jax.random.normal(key, extent, jnp.float32)
    if pieces:
        result = result * shard_levels(key, extent, pieces, -0.22, 0.18)
    return jnp.clip(result, -bound, bound).astype(held_as)


def setup_inputs(seed: int = 0) -> dict:
    key_list = jax.random.split(jax.random.key(seed), 8)
    features_t = scatter_about(key_list[0], (F, NODES), 1.0, 6.0, ((0, 4), (1, 32)))
    tile_values = jnp.clip(0.015319824 * jax.random.uniform(key_list[1], (N_BLK, N_BLK, TPS, TILE, TILE), jnp.float32) ** shard_levels(key_list[1], (N_BLK, N_BLK, TPS, TILE, TILE), ((0, 32),), -0.2, 0.2), 0.0, 0.015319824).astype(jnp.bfloat16)
    tile_rows = set_ends(jax.random.randint(key_list[2], (N_BLK, N_BLK, TPS), 0, BLOCKS), jax.random.fold_in(key_list[2], 1), 0, BLOCKS - 1).astype(jnp.int32)
    tile_cols = set_ends(jax.random.randint(key_list[3], (N_BLK, N_BLK, TPS), 0, BLOCKS), jax.random.fold_in(key_list[3], 1), 0, BLOCKS - 1).astype(jnp.int32)
    tile_count = draw_tile_count(jax.random.fold_in(key_list[7], 71), 0)
    weight = scatter_about(key_list[5], (F, H), F ** -0.5, 0.375, ((0, 4),))
    cotangent_t = scatter_about(key_list[6], (H, NODES), 1.0, 6.0, ((0, 4), (1, 32)))
    return {"features_t": features_t, "tile_values": tile_values, "tile_rows": tile_rows, "tile_cols": tile_cols, "tile_count": tile_count, "weight": weight, "cotangent_t": cotangent_t}


def blocks_of(field):
    return field.reshape(field.shape[0], N_BLK, BLOCKS, TILE)


def reference(features_t, tile_values, tile_rows, tile_cols, tile_count, weight, cotangent_t):
    section_ids = jnp.arange(N_BLK, dtype=jnp.int32)
    slot_ids = jnp.arange(TPS, dtype=jnp.int32)
    level_ids = jnp.arange(BLOCKS, dtype=jnp.int32)
    source_blocks = blocks_of(features_t.astype(jnp.float32))

    def forward_part(partition):
        source_parts = (partition - section_ids) % N_BLK
        live_mask = (slot_ids[None, :] < tile_count[partition][:, None]).astype(jnp.float32)
        picked = source_blocks[:, source_parts[:, None], tile_cols[partition], :]
        products = jnp.einsum("fktj,ktij->ktfi", picked, tile_values[partition].astype(jnp.float32))
        placement = (tile_rows[partition][:, :, None] == level_ids).astype(jnp.float32) * live_mask[:, :, None]
        return jnp.einsum("ktb,ktfi->fbi", placement, products)

    aggregated = lax.map(forward_part, jnp.arange(N_BLK, dtype=jnp.int32))
    aggregated_t = jnp.transpose(aggregated, (1, 0, 2, 3)).reshape(F, NODES).astype(jnp.bfloat16)
    pre_act = jnp.dot(weight.T, aggregated_t, preferred_element_type=jnp.float32)
    sigmoid_pre = jax.nn.sigmoid(pre_act)
    hidden_t = (pre_act * sigmoid_pre).astype(jnp.bfloat16)
    pre_grad = (cotangent_t.astype(jnp.float32) * sigmoid_pre * (1.0 + pre_act * (1.0 - sigmoid_pre))).astype(jnp.bfloat16)
    weight_grad = jnp.dot(aggregated_t, pre_grad.T, preferred_element_type=jnp.float32) * (NODES ** -0.5)
    signal_t = jnp.dot(weight, pre_grad, preferred_element_type=jnp.float32).astype(jnp.bfloat16)
    signal_blocks = blocks_of(signal_t.astype(jnp.float32))

    def backward_part(partition, grad_blocks):
        source_parts = (partition - section_ids) % N_BLK
        live_mask = (slot_ids[None, :] < tile_count[partition][:, None]).astype(jnp.float32)
        own_blocks = lax.dynamic_index_in_dim(signal_blocks, partition, 1, False)
        picked = own_blocks[:, tile_rows[partition], :]
        products = jnp.einsum("fkti,ktij->ktfj", picked, tile_values[partition].astype(jnp.float32))
        products = products * live_mask[:, :, None, None]
        return grad_blocks.at[:, source_parts[:, None], tile_cols[partition], :].add(jnp.transpose(products, (2, 0, 1, 3)))

    grad_blocks = lax.fori_loop(0, N_BLK, backward_part, jnp.zeros((F, N_BLK, BLOCKS, TILE), jnp.float32))
    input_grad_t = grad_blocks.reshape(F, NODES).astype(jnp.bfloat16)
    return hidden_t, weight_grad, input_grad_t
```

```python
import jax
import jax.numpy as jnp
from jax import lax
from jax.experimental import pallas as pl
from jax.experimental.pallas import tpu as pltpu
from jax.sharding import PartitionSpec as P

MESH = pl.DeviceIdType.MESH
BF16, F32 = jnp.bfloat16, jnp.float32
RING = 8
SIDE = 4
SLOTS = 12
TILE = 128
ROWS = 64
NODES = 512
PARTS = 32
HALF = ROWS // 2

ORDER = [(d, cc) for d in (0, 1, 7, 2, 6, 3, 5, 4) for cc in (0, 1)]
PLACE = {pair: n for n, pair in enumerate(ORDER)}


def kernel(
    feat, tiles, tile_rows, tile_cols, tile_count, weight, cot,
    hid, wgrad, igrad,
    raw, acc, dense, panels, agg, w_all, w_turned, cot_all,
    agg_out, agg_in, hid_out, sig_out, sig_in,
    g1_out, g1, g2_out, g2, g3_out, g3, g4_out,
    back_out, back_in, keep, chain_out, chain_in, fin_out, fin_in, done,
    tile_sem, local_sem, hop_sem, ring_send, ring_recv, core_send, core_recv,
    w_send, w_recv, cot_send, cot_recv, agg_send, agg_recv, sig_send, sig_recv,
    hid_send, hid_recv, g1_send, g1_recv, g2_send, g2_recv, g3_send, g3_recv, g4_send, g4_recv,
    back_send, back_recv, chain_send, chain_recv, fin_send, fin_recv,
):
    p, r, f = lax.axis_index("blk"), lax.axis_index("rep"), lax.axis_index("feat")
    z, xh, c = p // 4, (p // 2) % 2, p % 2

    def at(dz=0, dx=0, dc=0, dr=0, df=0):
        nz = (z + dz) % RING
        nx, nc, nr = (xh + dx) % 2, (c + dc) % 2, (r + dr) % 2
        return (nz * 4 + nx * 2 + nc, nr, (f + df) % SIDE)

    def remote(src, dst, send, recv, device):
        return pltpu.make_async_remote_copy(
            src_ref=src, dst_ref=dst, send_sem=send, recv_sem=recv, device_id=device, device_id_type=MESH
        )

    def tile_copy(n):
        half = n // 2
        odd, step = half % 2, (half + 1) // 2
        d = (odd * step + (1 - odd) * (RING - step)) % RING
        source = ((z + RING - d) % RING) * 4 + ((xh + r) % 2) * 2 + (c + n % 2) % 2
        section = (p + PARTS - source) % PARTS
        return section, pltpu.make_async_copy(tiles.at[0, section], raw.at[n], tile_sem.at[n])

    own_feat = pltpu.make_async_copy(feat, panels.at[0, 0], local_sem.at[0])
    own_w = pltpu.make_async_copy(weight, w_all.at[f], local_sem.at[1])
    own_lanes = pl.ds(pl.multiple_of(f * TILE, TILE), TILE)
    own_cot = pltpu.make_async_copy(cot.at[:, own_lanes], cot_all.at[f], local_sem.at[2])

    @pl.when(r == 0)
    def _():
        own_feat.start()

    own_w.start()
    own_cot.start()

    def start_tiles(n, carried):
        tile_copy(n)[1].start()
        return carried

    lax.fori_loop(0, 16, start_tiles, 0)

    partners = [at(dz=dz) for dz in range(1, RING)]
    partners += [at(dx=i // 4, dc=(i // 2) % 2, dr=i % 2) for i in range(1, 8)]
    partners += [at(dr=dr, df=df) for dr in range(2) for df in range(1, SIDE)]
    barrier = pltpu.get_barrier_semaphore()
    for device in partners:
        pl.semaphore_signal(barrier, inc=1, device_id=device, device_id_type=MESH)
    acc[SLOTS] = jnp.zeros((TILE, TILE), BF16)
    agg[...] = jnp.zeros_like(agg)
    pl.semaphore_wait(barrier, len(partners))

    hop = remote(panels.at[0, 0], panels.at[0, 0], hop_sem.at[0], hop_sem.at[1], at(dx=1, dr=1))

    @pl.when(r == 0)
    def _():
        own_feat.wait()
        hop.start()

    @pl.when(r == 1)
    def _():
        hop.wait_recv()

    def ring_copy(way, step, chunk):
        d = step if way == 0 else (RING - step) % RING
        to = d + 1 if way == 0 else RING - 1 - step
        span = pl.ds(chunk * HALF, HALF)
        return remote(
            panels.at[d, 0, span], panels.at[to, 0, span],
            ring_send.at[way, step, chunk], ring_recv.at[way, step, chunk],
            at(dz=1 if way == 0 else RING - 1),
        )

    def core_copy(d):
        return remote(panels.at[d, 0], panels.at[d, 1], core_send.at[d], core_recv.at[d], at(dc=1))

    for chunk in range(2):
        for way in range(2):
            ring_copy(way, 0, chunk).start()
    core_copy(0).start()

    def w_copy(df):
        return remote(weight, w_all.at[f], w_send.at[df], w_recv.at[df], at(df=df))

    def cot_copy(df):
        lanes = pl.ds(pl.multiple_of(((f + df) % SIDE) * TILE, TILE), TILE)
        return remote(cot.at[:, lanes], cot_all.at[f], cot_send.at[df], cot_recv.at[df], at(df=df))

    for df in range(1, SIDE):
        w_copy(df).start()
        cot_copy(df).start()

    def densify(n, carried):
        section, copy = tile_copy(n)
        copy.wait()
        live = tile_count[0, section]
        target = [
            jnp.where(t < live, tile_rows[0, section, t] * SIDE + tile_cols[0, section, t], 16)
            for t in range(SLOTS)
        ]
        for t in range(SLOTS):
            before = jnp.int32(SLOTS)
            for u in range(t):
                before = jnp.where(target[u] == target[t], u, before)
            acc[t] = raw[n, t] + acc[before]
        for b in range(16):
            last = jnp.int32(SLOTS)
            for t in range(SLOTS):
                last = jnp.where(target[t] == b, t, last)
            i, j = b // SIDE, b % SIDE
            dense[n, i * TILE:(i + 1) * TILE, j * TILE:(j + 1) * TILE] = acc[last]
        return carried

    def forward(d, cc):
        if cc:
            core_copy(d).wait_recv()
        agg[...] += lax.dot_general(
            panels[d, cc], dense[PLACE[d, cc]], (((1,), (1,)), ((), ())), preferred_element_type=F32
        )

    lax.fori_loop(0, 4, densify, 0)
    for step in range(4):
        for chunk in range(2):
            for way in range(2):
                if step < 3 or chunk == way:
                    ring_copy(way, step, chunk).wait_recv()
                    if step < 2 or (step == 2 and chunk == way):
                        ring_copy(way, step + 1, chunk).start()
        core_copy(step + 1).start()
        if step < 3:
            core_copy(RING - 1 - step).start()
            lax.fori_loop(4 * step + 4, 4 * step + 8, densify, 0)
        if step == 0:
            forward(0, 0)
            forward(0, 1)
        else:
            for d in (step, RING - step):
                forward(d, 0)
                forward(d, 1)
        if step == 2:
            own_w.wait()
            for df in range(1, SIDE):
                w_copy(df).wait_recv()
            w_turned[...] = w_all[...].reshape(256, 256).astype(F32).T.astype(BF16)
    forward(4, 0)
    forward(4, 1)

    def agg_copy(dr, df):
        return remote(
            agg_out.at[(f + df) % SIDE], agg_in.at[r, f], agg_send.at[dr, df], agg_recv.at[dr, df], at(dr=dr, df=df)
        )

    group = [(dr, df) for df in (2, 1, 3, 0) for dr in (1, 0) if dr or df]
    for b in range(SIDE):
        agg_out[b] = agg[:, b * TILE:(b + 1) * TILE].astype(BF16)
    for dr, df in group:
        agg_copy(dr, df).start()
    agg_in[r, f] = agg_out[f]
    own_cot.wait()
    for df in range(1, SIDE):
        cot_copy(df).wait_recv()
    for dr, df in group:
        agg_copy(dr, df).wait_recv()
    summed = (agg_in[0].astype(F32) + agg_in[1].astype(F32)).reshape(256, TILE).astype(BF16)
    pre_act = jnp.dot(w_turned[...], summed, preferred_element_type=F32)
    gate = 1.0 / (1.0 + jnp.exp(-pre_act))
    grad = cot_all[...].reshape(256, TILE).astype(F32)
    pre_grad = (grad * gate * (1.0 + pre_act * (1.0 - gate))).astype(BF16)
    signal = jnp.dot(w_all[...].reshape(256, 256), pre_grad, preferred_element_type=F32)
    sig_out[...] = signal.astype(BF16).reshape(SIDE, ROWS, TILE)

    def sig_copy(df):
        return remote(sig_out.at[(f + df) % SIDE], sig_in.at[f], sig_send.at[df], sig_recv.at[df], at(df=df))

    for df in (2, 1, 3):
        sig_copy(df).start()
    sig_in[f] = sig_out[f]

    hid_out[...] = (pre_act * gate).astype(BF16).reshape(SIDE, ROWS, TILE)

    def hid_copy(df):
        return remote(
            hid_out.at[(f + df) % SIDE], hid.at[:, own_lanes], hid_send.at[df], hid_recv.at[df], at(df=df)
        )

    own_hid = pltpu.make_async_copy(hid_out.at[f], hid.at[:, own_lanes], local_sem.at[3])
    own_hid.start()
    for df in range(1, SIDE):
        hid_copy(df).start()
    grad_rows = jnp.where(r == 0, pre_grad[:TILE].astype(F32), pre_grad[TILE:].astype(F32)).astype(BF16)
    share = lax.dot_general(summed, grad_rows, (((1,), (1,)), ((), ())), preferred_element_type=F32)
    g1_out[...] = share.reshape(SIDE, ROWS, TILE)

    def g1_copy(df):
        return remote(g1_out.at[(f + df) % SIDE], g1.at[f], g1_send.at[df], g1_recv.at[df], at(df=df))

    for df in range(1, SIDE):
        g1_copy(df).start()
    g1[f] = g1_out[f]

    for df in (2, 1, 3):
        sig_copy(df).wait_recv()
    signal_row = jnp.concatenate([sig_in[b] for b in range(SIDE)], axis=1)

    def backward(d, cc):
        return jnp.dot(signal_row, dense[PLACE[d, cc]], preferred_element_type=F32)

    def back_copy(d):
        return remote(back_out.at[d], back_in.at[d], back_send.at[d], back_recv.at[d], at(dc=1))

    def give(d):
        back_out[d] = backward(d, 1).astype(BF16)
        back_copy(d).start()

    def take(d):
        keep[d] = backward(d, 0)
        back_copy(d).wait_recv()
        keep[d] += back_in[d].astype(F32)

    def chain_copy(way, level, chunk):
        span = pl.ds(chunk * HALF, HALF)
        return remote(
            chain_out.at[way, level - 1, span], chain_in.at[way, level - 1, span],
            chain_send.at[way, level - 1, chunk], chain_recv.at[way, level - 1, chunk],
            at(dz=RING - 1 if way == 0 else 1),
        )

    def pass_on(way, level, chunk):
        d = level if way == 0 else RING - level
        rows = slice(chunk * HALF, (chunk + 1) * HALF)
        value = keep[d, rows]
        if level < 3 or (level == 3 and chunk != way):
            chain_copy(way, level + 1, chunk).wait_recv()
            value = value + chain_in[way, level, rows].astype(F32)
        chain_out[way, level - 1, rows] = value.astype(BF16)
        chain_copy(way, level, chunk).start()

    give(4)
    give(3)
    give(5)
    take(4)
    pass_on(0, 4, 1)
    pass_on(1, 4, 0)
    give(2)
    give(6)
    take(3)
    pass_on(0, 3, 0)
    take(5)
    pass_on(1, 3, 1)
    pass_on(0, 3, 1)
    pass_on(1, 3, 0)

    for df in range(1, SIDE):
        g1_copy(df).wait_recv()
    g2_out[...] = (g1[0] + g1[1]) + (g1[2] + g1[3])

    def g2_copy(dz):
        rows = pl.ds(pl.multiple_of(((z + dz) % RING) * 8, 8), 8)
        return remote(g2_out.at[rows], g2.at[z], g2_send.at[dz], g2_recv.at[dz], at(dz=dz))

    for dz in range(1, RING):
        g2_copy(dz).start()
    g2[z] = g2_out[pl.ds(pl.multiple_of(z * 8, 8), 8)]

    give(1)
    give(7)
    take(2)
    take(6)
    for chunk in range(2):
        pass_on(0, 2, chunk)
        pass_on(1, 2, 1 - chunk)

    for dz in range(1, RING):
        g2_copy(dz).wait_recv()
    g3_out[...] = jnp.sum(g2[...], axis=0)

    def g3_copy(i):
        return remote(
            g3_out, g3.at[r * 4 + xh * 2 + c], g3_send.at[i], g3_recv.at[i],
            at(dx=i // 4, dc=(i // 2) % 2, dr=i % 2),
        )

    for i in range(1, 8):
        g3_copy(i).start()
    g3[r * 4 + xh * 2 + c] = g3_out[...]

    give(0)
    take(1)
    take(7)
    for chunk in range(2):
        pass_on(0, 1, chunk)
        pass_on(1, 1, 1 - chunk)

    for i in range(1, 8):
        g3_copy(i).wait_recv()
    scale = float(NODES * PARTS) ** -0.5
    for half in range(2):
        four = (g3[4 * half] + g3[4 * half + 1]) + (g3[4 * half + 2] + g3[4 * half + 3])
        g4_out[:, half * TILE:(half + 1) * TILE] = four * scale
    own_rows = pl.ds(pl.multiple_of(z * 8, 8), 8)

    def g4_copy(dz):
        return remote(g4_out, wgrad.at[own_rows], g4_send.at[dz], g4_recv.at[dz], at(dz=dz))

    for dz in range(1, RING):
        g4_copy(dz).start()
    own_wgrad = pltpu.make_async_copy(g4_out, wgrad.at[own_rows], local_sem.at[4])
    own_wgrad.start()

    take(0)

    def fin_copy(i, chunk):
        span = pl.ds(chunk * HALF, HALF)
        device = (at(dr=1), at(dx=1, dr=1), at(dx=1))[i]
        return remote(
            fin_out.at[span], fin_in.at[min(i, 1), span], fin_send.at[i, chunk], fin_recv.at[min(i, 1), chunk], device
        )

    for chunk in range(2):
        rows = slice(chunk * HALF, (chunk + 1) * HALF)
        value = keep[0, rows]
        for way in range(2):
            chain_copy(way, 1, chunk).wait_recv()
            value = value + chain_in[way, 0, rows].astype(F32)
        fin_out[rows] = value.astype(BF16)

        @pl.when(r == 0)
        def _():
            fin_copy(0, chunk).start()

        @pl.when(r == 1)
        def _():
            fin_copy(2, chunk).start()
            fin_copy(1, chunk).start()

    for chunk in range(2):
        rows = slice(chunk * HALF, (chunk + 1) * HALF)
        fin_copy(1, chunk).wait_recv()

        @pl.when(r == 0)
        def _():
            fin_in[0, rows] = fin_out[rows]

        @pl.when(r == 1)
        def _():
            fin_copy(0, chunk).wait_recv()

        done[rows] = (fin_in[0, rows].astype(F32) + fin_in[1, rows].astype(F32)).astype(BF16)
    own_igrad = pltpu.make_async_copy(done, igrad, local_sem.at[5])
    own_igrad.start()

    @pl.when(r == 0)
    def _():
        hop.wait_send()
        for chunk in range(2):
            fin_copy(0, chunk).wait_send()

    @pl.when(r == 1)
    def _():
        for chunk in range(2):
            fin_copy(1, chunk).wait_send()
            fin_copy(2, chunk).wait_send()

    for way in range(2):
        for step in range(4):
            for chunk in range(2):
                if step < 3 or chunk == way:
                    ring_copy(way, step, chunk).wait_send()
        for level in range(1, 5):
            for chunk in range(2):
                if level < 4 or chunk != way:
                    chain_copy(way, level, chunk).wait_send()
    for d in range(RING):
        core_copy(d).wait_send()
        back_copy(d).wait_send()
    for dr, df in group:
        agg_copy(dr, df).wait_send()
    for df in range(1, SIDE):
        w_copy(df).wait_send()
        cot_copy(df).wait_send()
        sig_copy(df).wait_send()
        g1_copy(df).wait_send()
        hid_copy(df).wait()
    for dz in range(1, RING):
        g2_copy(dz).wait_send()
        g3_copy(dz).wait_send()
        g4_copy(dz).wait()
    own_hid.wait()
    own_wgrad.wait()
    own_igrad.wait()


def body(features_t, tile_values, tile_rows, tile_cols, tile_count, weight, cotangent_t):
    anywhere = pl.BlockSpec(memory_space=pl.ANY)
    scalars = pl.BlockSpec(memory_space=pltpu.SMEM)
    vmem, dma = pltpu.VMEM, pltpu.SemaphoreType.DMA
    block = (SIDE, ROWS, TILE)
    panel = (ROWS, NODES)
    return pl.pallas_call(
        kernel,
        out_shape=(
            jax.ShapeDtypeStruct((ROWS, NODES), BF16),
            jax.ShapeDtypeStruct((ROWS, 256), F32),
            jax.ShapeDtypeStruct((ROWS, NODES), BF16),
        ),
        in_specs=[anywhere, anywhere, scalars, scalars, scalars, anywhere, anywhere],
        out_specs=(anywhere, anywhere, anywhere),
        scratch_shapes=[
            vmem((16, SLOTS, TILE, TILE), BF16),
            vmem((SLOTS + 1, TILE, TILE), BF16),
            vmem((16, NODES, NODES), BF16),
            vmem((RING, 2, *panel), BF16),
            vmem(panel, F32),
            vmem((SIDE, ROWS, 256), BF16),
            vmem((256, 256), BF16),
            vmem(block, BF16),
            vmem(block, BF16),
            vmem((2, *block), BF16),
            vmem(block, BF16),
            vmem(block, BF16),
            vmem(block, BF16),
            vmem(block, F32),
            vmem(block, F32),
            vmem((ROWS, TILE), F32),
            vmem((RING, 8, TILE), F32),
            vmem((8, TILE), F32),
            vmem((8, 8, TILE), F32),
            vmem((8, 256), F32),
            vmem((RING, *panel), BF16),
            vmem((RING, *panel), BF16),
            vmem((RING, *panel), F32),
            vmem((2, 4, *panel), BF16),
            vmem((2, 4, *panel), BF16),
            vmem(panel, BF16),
            vmem((2, *panel), BF16),
            vmem(panel, BF16),
            dma((16,)), dma((6,)), dma((2,)),
            dma((2, 4, 2)), dma((2, 4, 2)), dma((RING,)), dma((RING,)),
            dma((SIDE,)), dma((SIDE,)), dma((SIDE,)), dma((SIDE,)),
            dma((2, SIDE)), dma((2, SIDE)), dma((SIDE,)), dma((SIDE,)),
            dma((SIDE,)), dma((SIDE,)), dma((SIDE,)), dma((SIDE,)),
            dma((RING,)), dma((RING,)), dma((8,)), dma((8,)), dma((RING,)), dma((RING,)),
            dma((RING,)), dma((RING,)), dma((2, 4, 2)), dma((2, 4, 2)), dma((3, 2)), dma((2, 2)),
        ],
        compiler_params=pltpu.CompilerParams(
            collective_id=0, has_side_effects=True, vmem_limit_bytes=40 * 1024 * 1024
        ),
    )(features_t, tile_values, tile_rows, tile_cols, tile_count, weight, cotangent_t)


def solution(mesh):
    return jax.shard_map(
        body,
        mesh=mesh,
        in_specs=(
            P("feat", "blk"),
            P("blk", None, None, None, None),
            P("blk", None, None),
            P("blk", None, None),
            P("blk", None),
            P("feat", None),
            P("feat", "blk"),
        ),
        out_specs=(P("feat", "blk"), P("feat", None), P("feat", "blk")),
        check_vma=False,
    )
```

```python
import jax
import jax.numpy as jnp
from jax import lax
from jax.experimental import pallas as pl
from jax.experimental.pallas import tpu as pltpu
from jax.sharding import PartitionSpec as P

MESH = pl.DeviceIdType.MESH
BF16, F32 = jnp.bfloat16, jnp.float32
RING = 8
SIDE = 4
SLOTS = 12
TILE = 128
ROWS = 64
NODES = 512
PARTS = 32
HALF = ROWS // 2
VMEM_BYTES = 62 * 1024 * 1024

ORDER = [(d, cc) for d in (0, 1, 7, 2, 6, 3, 5, 4) for cc in (0, 1)]
PLACE = {pair: n for n, pair in enumerate(ORDER)}
DIRECT = {2: 0, 6: 1, 1: 2, 7: 3, 0: 4}


def kernel(
    feat, tiles, rows_hbm, cols_hbm, count_hbm, weight, cot,
    hid, wgrad, igrad,
    tile_rows, tile_cols, tile_count,
    raw, acc, dense, panels, agg, w_all, w_turned, cot_all,
    agg_out, agg_in, hid_out, sig_out, sig_in,
    g1_out, g1, g2_out, g2, g3_out, g3, g4_out,
    back_out, back_in, keep, near_out, near_in, root_out, root_in, done,
    tile_sem, local_sem, first_send, first_recv, second_send, second_recv, core_send, core_recv,
    w_send, w_recv, cot_send, cot_recv, agg_send, agg_recv, sig_send, sig_recv,
    hid_send, hid_recv, g1_send, g1_recv, g2_send, g2_recv, g3_send, g3_recv, g4_send, g4_recv,
    back_send, back_recv, near_send, near_recv, root_send, root_recv, fin_send, fin_recv,
):
    p, r, f = lax.axis_index("blk"), lax.axis_index("rep"), lax.axis_index("feat")
    z, xh, c = p // 4, (p // 2) % 2, p % 2
    lane = (c + r) % 2

    def at(dz=0, dx=0, dc=0, dr=0, df=0):
        nz = (z + dz) % RING
        nx, nc, nr = (xh + dx) % 2, (c + dc) % 2, (r + dr) % 2
        return (nz * 4 + nx * 2 + nc, nr, (f + df) % SIDE)

    pending = []

    def go(copy):
        copy.start()
        pending.append(copy)

    def remote(src, dst, send, recv, device):
        return pltpu.make_async_remote_copy(
            src_ref=src, dst_ref=dst, send_sem=send, recv_sem=recv, device_id=device, device_id_type=MESH
        )

    def tile_copy(n):
        half = n // 2
        odd, step = half % 2, (half + 1) // 2
        d = (odd * step + (1 - odd) * (RING - step)) % RING
        source = ((z + RING - d) % RING) * 4 + ((xh + lane + n % 2) % 2) * 2 + r
        section = (p + PARTS - source) % PARTS
        return section, pltpu.make_async_copy(tiles.at[0, section], raw.at[n], tile_sem.at[n])

    own_feat = pltpu.make_async_copy(feat, panels.at[0, 0], local_sem.at[0])
    own_w = pltpu.make_async_copy(weight, w_all.at[f], local_sem.at[1])
    own_lanes = pl.ds(pl.multiple_of(f * TILE, TILE), TILE)
    own_cot = pltpu.make_async_copy(cot.at[:, own_lanes], cot_all.at[f], local_sem.at[2])

    scalar_copies = [
        pltpu.make_async_copy(src, dst, local_sem.at[3 + i])
        for i, (src, dst) in enumerate(((rows_hbm, tile_rows), (cols_hbm, tile_cols), (count_hbm, tile_count)))
    ]
    for copy in scalar_copies:
        copy.start()

    @pl.when(lane == 0)
    def _():
        own_feat.start()

    own_w.start()
    own_cot.start()

    def start_tiles(n, carried):
        tile_copy(n)[1].start()
        return carried

    lax.fori_loop(0, 16, start_tiles, 0)

    partners = [at(dz=dz) for dz in (4, 3, 5, 2, 6, 1, 7)]
    partners += [at(dz=dz, dx=1, dc=1) for dz in (2, 6, 1, 7, 0)]
    partners += [at(dr=dr, df=df) for df in (2, 1, 3, 0) for dr in range(2) if dr or df]
    partners += [at(dc=1), at(dx=1), at(dx=1, dr=1), at(dc=1, dr=1), at(dx=1, dc=1, dr=1)]
    barrier = pltpu.get_barrier_semaphore()
    for device in partners:
        pl.semaphore_signal(barrier, inc=1, device_id=device, device_id_type=MESH)
    acc[SLOTS] = jnp.zeros((TILE, TILE), BF16)
    agg[...] = jnp.zeros_like(agg)
    pl.semaphore_wait(barrier, len(partners))

    def first_copy(to_lane, d, chunk):
        span = pl.ds(chunk * HALF, HALF) if d in (2, 6) else pl.ds(0, ROWS)
        return remote(
            feat.at[span], panels.at[d, 0, span],
            first_send.at[to_lane, DIRECT[d], chunk], first_recv.at[DIRECT[d], chunk],
            at(dz=d, dx=to_lane, dc=to_lane),
        )

    firsts = [(to_lane, d, i ^ (d == 6)) for i in range(2) for d in (2, 6) for to_lane in (1, 0)]
    firsts += [(to_lane, d, 0) for d in (1, 7) for to_lane in (1, 0)] + [(1, 0, 0)]

    @pl.when(lane == 0)
    def _():
        for first in firsts:
            first_copy(*first).start()

    def second_copy(way, part):
        d = 2 if way == 0 else RING - 2
        step = 2 if part == 2 else 1
        to = d + step if way == 0 else d - step
        chunk = part if part < 2 else way
        span = pl.ds(chunk * HALF, HALF)
        return remote(
            panels.at[d, 0, span], panels.at[to, 0, span],
            second_send.at[way, part], second_recv.at[way, part], at(dz=step if way == 0 else RING - step),
        )

    def core_copy(d):
        return remote(panels.at[d, 0], panels.at[d, 1], core_send.at[d], core_recv.at[d], at(dc=1))

    def w_copy(df):
        return remote(weight, w_all.at[f], w_send.at[df], w_recv.at[df], at(df=df))

    def cot_copy(df):
        lanes = pl.ds(pl.multiple_of(((f + df) % SIDE) * TILE, TILE), TILE)
        return remote(cot.at[:, lanes], cot_all.at[f], cot_send.at[df], cot_recv.at[df], at(df=df))

    for df in range(1, SIDE):
        go(w_copy(df))
        go(cot_copy(df))

    def densify(n, carried):
        section, copy = tile_copy(n)
        copy.wait()
        live = tile_count[0, section]
        target = [
            jnp.where(t < live, tile_rows[t, 0, section] * SIDE + tile_cols[t, 0, section], 16)
            for t in range(SLOTS)
        ]
        for t in range(SLOTS):
            before = jnp.int32(SLOTS)
            for u in range(t):
                before = jnp.where(target[u] == target[t], u, before)
            acc[t] = raw[n, t] + acc[before]
        for b in range(16):
            last = jnp.int32(SLOTS)
            for t in range(SLOTS):
                last = jnp.where(target[t] == b, t, last)
            i, j = b // SIDE, b % SIDE
            dense[n, i * TILE:(i + 1) * TILE, j * TILE:(j + 1) * TILE] = acc[last]
        return carried

    def forward(d, cc):
        if cc:
            core_copy(d).wait_recv()
        agg[...] += lax.dot_general(
            panels[d, cc], dense[PLACE[d, cc]], (((1,), (1,)), ((), ())), preferred_element_type=F32
        )

    for copy in scalar_copies:
        copy.wait()
    lax.fori_loop(0, 16, densify, 0)
    for i in range(2):
        for way in range(2):
            chunk = i ^ way
            first_copy(0, 2 if way == 0 else 6, chunk).wait_recv()
            if i == 0:
                go(second_copy(way, 2))
            go(second_copy(way, chunk))
    go(core_copy(2))
    go(core_copy(6))
    for d in (1, 7):
        first_copy(0, d, 0).wait_recv()
        go(core_copy(d))

    @pl.when(lane == 0)
    def _():
        own_feat.wait()

    @pl.when(lane == 1)
    def _():
        first_copy(1, 0, 0).wait_recv()

    go(core_copy(0))
    for d in (2, 6, 1, 7, 0):
        forward(d, 0)
        forward(d, 1)
    own_w.wait()
    for df in range(1, SIDE):
        w_copy(df).wait_recv()
    w_turned[...] = w_all[...].reshape(256, 256).astype(F32).T.astype(BF16)
    for way in range(2):
        second_copy(way, 0).wait_recv()
        second_copy(way, 1).wait_recv()
        go(core_copy(3 if way == 0 else 5))
    for way in range(2):
        second_copy(way, 2).wait_recv()
    go(core_copy(4))
    for d in (3, 5, 4):
        forward(d, 0)
    for d in (3, 5, 4):
        forward(d, 1)

    def agg_copy(dr, df):
        return remote(
            agg_out.at[(f + df) % SIDE], agg_in.at[r, f], agg_send.at[dr, df], agg_recv.at[dr, df], at(dr=dr, df=df)
        )

    group = [(dr, df) for df in (2, 1, 3, 0) for dr in (1, 0) if dr or df]
    for b in range(SIDE):
        agg_out[b] = agg[:, b * TILE:(b + 1) * TILE].astype(BF16)
    for dr, df in group:
        go(agg_copy(dr, df))
    agg_in[r, f] = agg_out[f]
    own_cot.wait()
    for df in range(1, SIDE):
        cot_copy(df).wait_recv()
    for dr, df in group:
        agg_copy(dr, df).wait_recv()
    summed = (agg_in[0].astype(F32) + agg_in[1].astype(F32)).reshape(256, TILE).astype(BF16)
    pre_act = jnp.dot(w_turned[...], summed, preferred_element_type=F32)
    gate = 1.0 / (1.0 + jnp.exp(-pre_act))
    grad = cot_all[...].reshape(256, TILE).astype(F32)
    pre_grad = (grad * gate * (1.0 + pre_act * (1.0 - gate))).astype(BF16)
    signal = jnp.dot(w_all[...].reshape(256, 256), pre_grad, preferred_element_type=F32)
    sig_out[...] = signal.astype(BF16).reshape(SIDE, ROWS, TILE)

    def sig_copy(df):
        return remote(sig_out.at[(f + df) % SIDE], sig_in.at[f], sig_send.at[df], sig_recv.at[df], at(df=df))

    for df in (2, 1, 3):
        go(sig_copy(df))
    sig_in[f] = sig_out[f]

    hid_out[...] = (pre_act * gate).astype(BF16).reshape(SIDE, ROWS, TILE)

    def hid_copy(df):
        return remote(
            hid_out.at[(f + df) % SIDE], hid.at[:, own_lanes], hid_send.at[df], hid_recv.at[df], at(df=df)
        )

    own_hid = pltpu.make_async_copy(hid_out.at[f], hid.at[:, own_lanes], local_sem.at[6])
    own_hid.start()
    for df in range(1, SIDE):
        go(hid_copy(df))
    grad_rows = jnp.where(r == 0, pre_grad[:TILE].astype(F32), pre_grad[TILE:].astype(F32)).astype(BF16)
    share = lax.dot_general(summed, grad_rows, (((1,), (1,)), ((), ())), preferred_element_type=F32)
    g1_out[...] = share.reshape(SIDE, ROWS, TILE)

    def g1_copy(df):
        return remote(g1_out.at[(f + df) % SIDE], g1.at[f], g1_send.at[df], g1_recv.at[df], at(df=df))

    for df in range(1, SIDE):
        go(g1_copy(df))
    g1[f] = g1_out[f]

    for df in (2, 1, 3):
        sig_copy(df).wait_recv()
    signal_row = jnp.concatenate([sig_in[b] for b in range(SIDE)], axis=1)

    def backward(d, cc):
        return jnp.dot(signal_row, dense[PLACE[d, cc]], preferred_element_type=F32)

    def back_copy(d):
        return remote(back_out.at[d], back_in.at[d], back_send.at[d], back_recv.at[d], at(dc=1))

    def give(d):
        back_out[d] = backward(d, 1).astype(BF16)
        go(back_copy(d))

    def take(d):
        keep[d] = backward(d, 0)
        back_copy(d).wait_recv()
        keep[d] += back_in[d].astype(F32)

    def near_copy(way, part):
        d = 4 if part == 2 else (3 if way == 0 else 5)
        step = 2 if part == 2 else 1
        span = pl.ds((part if part < 2 else way) * HALF, HALF)
        return remote(
            near_out.at[way, step - 1, span], near_in.at[way, step - 1, span],
            near_send.at[way, part], near_recv.at[way, part], at(dz=RING - step if way == 0 else step),
        )

    def root_copy(d, chunk, from_lane):
        span = pl.ds(chunk * HALF, HALF) if d in (2, 6) else pl.ds(0, ROWS)
        return remote(
            root_out.at[DIRECT[d], span], root_in.at[from_lane, DIRECT[d], span],
            root_send.at[DIRECT[d], chunk], root_recv.at[from_lane, DIRECT[d], chunk],
            at(dz=RING - d, dx=from_lane, dc=from_lane),
        )

    halves = [slice(0, HALF), slice(HALF, ROWS)]
    for d in (4, 3, 5):
        give(d)
    take(4)
    for way in range(2):
        near_out[way, 1, halves[way]] = keep[4, halves[way]].astype(BF16)
        go(near_copy(way, 2))
    for way in range(2):
        take(3 if way == 0 else 5)
        near_out[way, 0] = keep[3 if way == 0 else 5].astype(BF16)
        go(near_copy(way, way))
        go(near_copy(way, 1 - way))
    for d in (1, 7, 0, 2, 6):
        give(d)

    for df in range(1, SIDE):
        g1_copy(df).wait_recv()
    g2_out[...] = (g1[0] + g1[1]) + (g1[2] + g1[3])

    def g2_copy(dz):
        rows = pl.ds(pl.multiple_of(((z + dz) % RING) * 8, 8), 8)
        return remote(g2_out.at[rows], g2.at[z], g2_send.at[dz], g2_recv.at[dz], at(dz=dz))

    for dz in range(1, RING):
        go(g2_copy(dz))
    g2[z] = g2_out[pl.ds(pl.multiple_of(z * 8, 8), 8)]

    for d in (1, 7):
        take(d)
        root_out[DIRECT[d]] = keep[d].astype(BF16)
        go(root_copy(d, 0, lane))
    take(0)

    @pl.when(lane == 1)
    def _():
        root_out[DIRECT[0]] = keep[0].astype(BF16)
        root_copy(0, 0, lane).start()

    take(2)
    take(6)

    for dz in range(1, RING):
        g2_copy(dz).wait_recv()
    g3_out[...] = jnp.sum(g2[...], axis=0)

    def g3_copy(i):
        return remote(
            g3_out, g3.at[r * 4 + xh * 2 + c], g3_send.at[i], g3_recv.at[i],
            at(dx=i // 4, dc=(i // 2) % 2, dr=i % 2),
        )

    for i in range(1, 8):
        go(g3_copy(i))
    g3[r * 4 + xh * 2 + c] = g3_out[...]

    for i in range(2):
        for way in range(2):
            chunk, d = i ^ way, 2 if way == 0 else 6
            value = keep[d, halves[chunk]]
            near_copy(way, chunk).wait_recv()
            value = value + near_in[way, 0, halves[chunk]].astype(F32)
            if i == 0:
                near_copy(way, 2).wait_recv()
                value = value + near_in[way, 1, halves[chunk]].astype(F32)
            root_out[DIRECT[d], halves[chunk]] = value.astype(BF16)
            go(root_copy(d, chunk, lane))

    for i in range(1, 8):
        g3_copy(i).wait_recv()
    scale = float(NODES * PARTS) ** -0.5
    for half in range(2):
        four = (g3[4 * half] + g3[4 * half + 1]) + (g3[4 * half + 2] + g3[4 * half + 3])
        g4_out[:, half * TILE:(half + 1) * TILE] = four * scale
    own_rows = pl.ds(pl.multiple_of(z * 8, 8), 8)

    def g4_copy(dz):
        return remote(g4_out, wgrad.at[own_rows], g4_send.at[dz], g4_recv.at[dz], at(dz=dz))

    for dz in range(1, RING):
        go(g4_copy(dz))
    own_wgrad = pltpu.make_async_copy(g4_out, wgrad.at[own_rows], local_sem.at[7])
    own_wgrad.start()

    def fin_copy(chunk):
        span = pl.ds(chunk * HALF, HALF)
        return remote(done.at[span], igrad.at[span], fin_send.at[chunk], fin_recv.at[chunk], at(dr=1))

    own_igrad = pltpu.make_async_copy(done, igrad, local_sem.at[8])

    @pl.when(lane == 0)
    def _():
        for from_lane in range(2):
            for d in (1, 7, 0) if from_lane else (1, 7):
                root_copy(d, 0, from_lane).wait_recv()
        for chunk in range(2):
            value = keep[0, halves[chunk]]
            for from_lane in range(2):
                for d in (1, 7, 0) if from_lane else (1, 7):
                    value = value + root_in[from_lane, DIRECT[d], halves[chunk]].astype(F32)
            for from_lane in range(2):
                for d in (2, 6):
                    root_copy(d, chunk, from_lane).wait_recv()
                    value = value + root_in[from_lane, DIRECT[d], halves[chunk]].astype(F32)
            done[halves[chunk]] = value.astype(BF16)
            fin_copy(chunk).start()
        own_igrad.start()

    @pl.when(lane == 1)
    def _():
        for chunk in range(2):
            fin_copy(chunk).wait_recv()

    @pl.when(lane == 0)
    def _():
        for first in firsts:
            first_copy(*first).wait_send()
        for chunk in range(2):
            fin_copy(chunk).wait_send()
        own_igrad.wait()

    @pl.when(lane == 1)
    def _():
        root_copy(0, 0, lane).wait_send()

    for copy in pending:
        copy.wait_send()
    for df in range(1, SIDE):
        hid_copy(df).wait_recv()
    for dz in range(1, RING):
        g4_copy(dz).wait_recv()
    own_hid.wait()
    own_wgrad.wait()


def hand_over(hid, wgrad, igrad, hid_to, wgrad_to, igrad_to, sems):
    copies = [
        pltpu.make_async_copy(src, dst, sems.at[i])
        for i, (src, dst) in enumerate(((hid, hid_to), (wgrad, wgrad_to), (igrad, igrad_to)))
    ]
    for copy in copies:
        copy.start()
    for copy in copies:
        copy.wait()


def body(features_t, tile_values, tile_rows, tile_cols, tile_count, weight, cotangent_t):
    anywhere = pl.BlockSpec(memory_space=pl.ANY)
    vmem, dma = pltpu.VMEM, pltpu.SemaphoreType.DMA
    block = (SIDE, ROWS, TILE)
    panel = (ROWS, NODES)
    out_shape = (
        jax.ShapeDtypeStruct((ROWS, NODES), BF16),
        jax.ShapeDtypeStruct((ROWS, 256), F32),
        jax.ShapeDtypeStruct((ROWS, NODES), BF16),
    )
    results = pl.pallas_call(
        kernel,
        out_shape=out_shape,
        in_specs=[anywhere] * 7,
        out_specs=(anywhere, anywhere, anywhere),
        scratch_shapes=[
            pltpu.SMEM((SLOTS, 1, PARTS), jnp.int32),
            pltpu.SMEM((SLOTS, 1, PARTS), jnp.int32),
            pltpu.SMEM((1, PARTS), jnp.int32),
            vmem((16, SLOTS, TILE, TILE), BF16),
            vmem((SLOTS + 1, TILE, TILE), BF16),
            vmem((16, NODES, NODES), BF16),
            vmem((RING, 2, *panel), BF16),
            vmem(panel, F32),
            vmem((SIDE, ROWS, 256), BF16),
            vmem((256, 256), BF16),
            vmem(block, BF16),
            vmem(block, BF16),
            vmem((2, *block), BF16),
            vmem(block, BF16),
            vmem(block, BF16),
            vmem(block, BF16),
            vmem(block, F32),
            vmem(block, F32),
            vmem((ROWS, TILE), F32),
            vmem((RING, 8, TILE), F32),
            vmem((8, TILE), F32),
            vmem((8, 8, TILE), F32),
            vmem((8, 256), F32),
            vmem((RING, *panel), BF16),
            vmem((RING, *panel), BF16),
            vmem((RING, *panel), F32),
            vmem((2, 2, *panel), BF16),
            vmem((2, 2, *panel), BF16),
            vmem((5, *panel), BF16),
            vmem((2, 5, *panel), BF16),
            vmem(panel, BF16),
            dma((16,)), dma((9,)), dma((2, 5, 2)), dma((5, 2)), dma((2, 3)), dma((2, 3)), dma((RING,)), dma((RING,)),
            dma((SIDE,)), dma((SIDE,)), dma((SIDE,)), dma((SIDE,)),
            dma((2, SIDE)), dma((2, SIDE)), dma((SIDE,)), dma((SIDE,)),
            dma((SIDE,)), dma((SIDE,)), dma((SIDE,)), dma((SIDE,)),
            dma((RING,)), dma((RING,)), dma((8,)), dma((8,)), dma((RING,)), dma((RING,)),
            dma((RING,)), dma((RING,)), dma((2, 3)), dma((2, 3)), dma((5, 2)), dma((2, 5, 2)), dma((2,)), dma((2,)),
        ],
        compiler_params=pltpu.CompilerParams(
            collective_id=0, has_side_effects=True, vmem_limit_bytes=VMEM_BYTES
        ),
    )(
        features_t, tile_values, jnp.transpose(tile_rows, (2, 0, 1)), jnp.transpose(tile_cols, (2, 0, 1)),
        tile_count, weight, cotangent_t,
    )
    return pl.pallas_call(
        hand_over,
        out_shape=out_shape,
        in_specs=[anywhere] * 3,
        out_specs=(anywhere,) * 3,
        scratch_shapes=[dma((3,))],
    )(*results)


def solution(mesh):
    return jax.shard_map(
        body,
        mesh=mesh,
        in_specs=(
            P("feat", "blk"),
            P("blk", None, None, None, None),
            P("blk", None, None),
            P("blk", None, None),
            P("blk", None),
            P("feat", None),
            P("feat", "blk"),
        ),
        out_specs=(P("feat", "blk"), P("feat", None), P("feat", "blk")),
        check_vma=False,
    )
```

```python
import jax
import jax.numpy as jnp
from jax import lax
from jax.experimental import pallas as pl
from jax.experimental.pallas import tpu as pltpu
from jax.sharding import PartitionSpec as P

MESH = pl.DeviceIdType.MESH
BF16, F32 = jnp.bfloat16, jnp.float32
RING = 8
SIDE = 4
SLOTS = 12
TILE = 128
ROWS = 64
NODES = 512
PARTS = 32
HALF = ROWS // 2
VMEM_BYTES = 62 * 1024 * 1024

ORDER = [(d, cc) for d in (0, 1, 7, 2, 6, 3, 5, 4) for cc in (0, 1)]
PLACE = {pair: n for n, pair in enumerate(ORDER)}
DIRECT = {2: 0, 6: 1, 1: 2, 7: 3, 0: 4}


def kernel(
    feat, tiles, rows_hbm, cols_hbm, count_hbm, weight, cot,
    hid, wgrad, igrad,
    tile_rows, tile_cols, tile_count,
    raw, acc, dense, panels, agg, w_all, w_turned, cot_all,
    agg_out, agg_in, hid_out, sig_out, sig_in,
    g1_out, g1, g2_out, g2, g3_out, g3, g4_out,
    back_out, back_in, keep, near_out, near_in, root_out, root_in, done,
    tile_sem, local_sem, first_send, first_recv, second_send, second_recv, core_send, core_recv,
    w_send, w_recv, cot_send, cot_recv, agg_send, agg_recv, sig_send, sig_recv,
    hid_send, hid_recv, g1_send, g1_recv, g2_send, g2_recv, g3_send, g3_recv, g4_send, g4_recv,
    back_send, back_recv, near_send, near_recv, root_send, root_recv, fin_send, fin_recv,
):
    p, r, f = lax.axis_index("blk"), lax.axis_index("rep"), lax.axis_index("feat")
    z, xh, c = p // 4, (p // 2) % 2, p % 2
    lane = (c + r) % 2

    def at(dz=0, dx=0, dc=0, dr=0, df=0):
        nz = (z + dz) % RING
        nx, nc, nr = (xh + dx) % 2, (c + dc) % 2, (r + dr) % 2
        return (nz * 4 + nx * 2 + nc, nr, (f + df) % SIDE)

    pending = []

    def go(copy):
        copy.start()
        pending.append(copy)

    def remote(src, dst, send, recv, device):
        return pltpu.make_async_remote_copy(
            src_ref=src, dst_ref=dst, send_sem=send, recv_sem=recv, device_id=device, device_id_type=MESH
        )

    partners = [at(dz=dz) for dz in (4, 3, 5, 2, 6, 1, 7)]
    partners += [at(dz=dz, dx=1, dc=1) for dz in (2, 6, 1, 7, 0)]
    partners += [at(dr=dr, df=df) for df in (2, 1, 3, 0) for dr in range(2) if dr or df]
    partners += [at(dc=1), at(dx=1), at(dx=1, dr=1), at(dc=1, dr=1), at(dx=1, dc=1, dr=1)]
    barrier = pltpu.get_barrier_semaphore()
    for device in partners:
        pl.semaphore_signal(barrier, inc=1, device_id=device, device_id_type=MESH)

    def tile_copy(n):
        half = n // 2
        odd, step = half % 2, (half + 1) // 2
        d = (odd * step + (1 - odd) * (RING - step)) % RING
        source = ((z + RING - d) % RING) * 4 + ((xh + lane + n % 2) % 2) * 2 + r
        section = (p + PARTS - source) % PARTS
        return section, pltpu.make_async_copy(tiles.at[0, section], raw.at[n], tile_sem.at[n])

    own_feat = pltpu.make_async_copy(feat, panels.at[0, 0], local_sem.at[0])
    own_w = pltpu.make_async_copy(weight, w_all.at[f], local_sem.at[1])
    own_lanes = pl.ds(pl.multiple_of(f * TILE, TILE), TILE)
    own_cot = pltpu.make_async_copy(cot.at[:, own_lanes], cot_all.at[f], local_sem.at[2])

    scalar_copies = [
        pltpu.make_async_copy(src, dst, local_sem.at[3 + i])
        for i, (src, dst) in enumerate(((rows_hbm, tile_rows), (cols_hbm, tile_cols), (count_hbm, tile_count)))
    ]
    for copy in scalar_copies:
        copy.start()

    @pl.when(lane == 0)
    def _():
        own_feat.start()

    own_w.start()
    own_cot.start()

    def start_tiles(n, carried):
        tile_copy(n)[1].start()
        return carried

    lax.fori_loop(0, 16, start_tiles, 0)

    acc[SLOTS] = jnp.zeros((TILE, TILE), BF16)
    agg[...] = jnp.zeros_like(agg)
    pl.semaphore_wait(barrier, len(partners))

    def first_copy(to_lane, d, chunk):
        span = pl.ds(chunk * HALF, HALF) if d in (2, 6) else pl.ds(0, ROWS)
        return remote(
            feat.at[span], panels.at[d, 0, span],
            first_send.at[to_lane, DIRECT[d], chunk], first_recv.at[DIRECT[d], chunk],
            at(dz=d, dx=to_lane, dc=to_lane),
        )

    firsts = [(to_lane, d, i ^ (d == 6)) for i in range(2) for d in (2, 6) for to_lane in (1, 0)]
    firsts += [(to_lane, d, 0) for d in (1, 7) for to_lane in (1, 0)] + [(1, 0, 0)]

    @pl.when(lane == 0)
    def _():
        for first in firsts:
            first_copy(*first).start()

    def second_copy(way, part):
        d = 2 if way == 0 else RING - 2
        step = 2 if part == 2 else 1
        to = d + step if way == 0 else d - step
        chunk = part if part < 2 else way
        span = pl.ds(chunk * HALF, HALF)
        return remote(
            panels.at[d, 0, span], panels.at[to, 0, span],
            second_send.at[way, part], second_recv.at[way, part], at(dz=step if way == 0 else RING - step),
        )

    def core_copy(d):
        return remote(panels.at[d, 0], panels.at[d, 1], core_send.at[d], core_recv.at[d], at(dc=1))

    def w_copy(df):
        return remote(weight, w_all.at[f], w_send.at[df], w_recv.at[df], at(df=df))

    def cot_copy(df):
        lanes = pl.ds(pl.multiple_of(((f + df) % SIDE) * TILE, TILE), TILE)
        return remote(cot.at[:, lanes], cot_all.at[f], cot_send.at[df], cot_recv.at[df], at(df=df))

    for df in range(1, SIDE):
        go(w_copy(df))
        go(cot_copy(df))

    def densify(n, carried):
        section, copy = tile_copy(n)
        copy.wait()
        live = tile_count[0, section]
        target = [
            jnp.where(t < live, tile_rows[t, 0, section] * SIDE + tile_cols[t, 0, section], 16)
            for t in range(SLOTS)
        ]
        for t in range(SLOTS):
            before = jnp.int32(SLOTS)
            for u in range(t):
                before = jnp.where(target[u] == target[t], u, before)
            acc[t] = raw[n, t] + acc[before]
        for b in range(16):
            last = jnp.int32(SLOTS)
            for t in range(SLOTS):
                last = jnp.where(target[t] == b, t, last)
            i, j = b // SIDE, b % SIDE
            dense[n, i * TILE:(i + 1) * TILE, j * TILE:(j + 1) * TILE] = acc[last]
        return carried

    def forward(d, cc):
        if cc:
            core_copy(d).wait_recv()
        agg[...] += lax.dot_general(
            panels[d, cc], dense[PLACE[d, cc]], (((1,), (1,)), ((), ())), preferred_element_type=F32
        )

    for copy in scalar_copies:
        copy.wait()
    lax.fori_loop(0, 16, densify, 0)
    for i in range(2):
        for way in range(2):
            chunk = i ^ way
            first_copy(0, 2 if way == 0 else 6, chunk).wait_recv()
            if i == 0:
                go(second_copy(way, 2))
            go(second_copy(way, chunk))
    go(core_copy(2))
    go(core_copy(6))
    for d in (1, 7):
        first_copy(0, d, 0).wait_recv()
        go(core_copy(d))

    @pl.when(lane == 0)
    def _():
        own_feat.wait()

    @pl.when(lane == 1)
    def _():
        first_copy(1, 0, 0).wait_recv()

    go(core_copy(0))
    for d in (2, 6, 1, 7, 0):
        forward(d, 0)
        forward(d, 1)
    own_w.wait()
    for df in range(1, SIDE):
        w_copy(df).wait_recv()
    w_turned[...] = w_all[...].reshape(256, 256).astype(F32).T.astype(BF16)
    for way in range(2):
        second_copy(way, 0).wait_recv()
        second_copy(way, 1).wait_recv()
        go(core_copy(3 if way == 0 else 5))
    for way in range(2):
        second_copy(way, 2).wait_recv()
    go(core_copy(4))
    for d in (3, 5, 4):
        forward(d, 0)
    for d in (3, 5, 4):
        forward(d, 1)

    def agg_copy(dr, df):
        return remote(
            agg_out.at[(f + df) % SIDE], agg_in.at[r, f], agg_send.at[dr, df], agg_recv.at[dr, df], at(dr=dr, df=df)
        )

    group = [(dr, df) for df in (2, 1, 3, 0) for dr in (1, 0) if dr or df]
    for b in range(SIDE):
        agg_out[b] = agg[:, b * TILE:(b + 1) * TILE].astype(BF16)
    for dr, df in group:
        go(agg_copy(dr, df))
    agg_in[r, f] = agg_out[f]
    own_cot.wait()
    for df in range(1, SIDE):
        cot_copy(df).wait_recv()
    for dr, df in group:
        agg_copy(dr, df).wait_recv()
    summed = (agg_in[0].astype(F32) + agg_in[1].astype(F32)).reshape(256, TILE).astype(BF16)
    pre_act = jnp.dot(w_turned[...], summed, preferred_element_type=F32)
    gate = 1.0 / (1.0 + jnp.exp(-pre_act))
    grad = cot_all[...].reshape(256, TILE).astype(F32)
    pre_grad = (grad * gate * (1.0 + pre_act * (1.0 - gate))).astype(BF16)
    signal = jnp.dot(w_all[...].reshape(256, 256), pre_grad, preferred_element_type=F32)
    sig_out[...] = signal.astype(BF16).reshape(SIDE, ROWS, TILE)

    def sig_copy(df):
        return remote(sig_out.at[(f + df) % SIDE], sig_in.at[f], sig_send.at[df], sig_recv.at[df], at(df=df))

    for df in (2, 1, 3):
        go(sig_copy(df))
    sig_in[f] = sig_out[f]

    grad_rows = jnp.where(r == 0, pre_grad[:TILE].astype(F32), pre_grad[TILE:].astype(F32)).astype(BF16)
    share = lax.dot_general(summed, grad_rows, (((1,), (1,)), ((), ())), preferred_element_type=F32)
    g1_out[...] = share.astype(BF16).reshape(SIDE, ROWS, TILE)

    def g1_copy(df):
        return remote(g1_out.at[(f + df) % SIDE], g1.at[f], g1_send.at[df], g1_recv.at[df], at(df=df))

    for df in range(1, SIDE):
        go(g1_copy(df))
    g1[f] = g1_out[f]

    hid_out[...] = (pre_act * gate).astype(BF16).reshape(SIDE, ROWS, TILE)

    def hid_copy(df):
        return remote(
            hid_out.at[(f + df) % SIDE], hid.at[:, own_lanes], hid_send.at[df], hid_recv.at[df], at(df=df)
        )

    own_hid = pltpu.make_async_copy(hid_out.at[f], hid.at[:, own_lanes], local_sem.at[6])
    own_hid.start()
    for df in range(1, SIDE):
        go(hid_copy(df))

    for df in (2, 1, 3):
        sig_copy(df).wait_recv()
    signal_row = jnp.concatenate([sig_in[b] for b in range(SIDE)], axis=1)

    def backward(d, cc):
        return jnp.dot(signal_row, dense[PLACE[d, cc]], preferred_element_type=F32)

    def back_copy(d):
        return remote(back_out.at[d], back_in.at[d], back_send.at[d], back_recv.at[d], at(dc=1))

    def give(d):
        back_out[d] = backward(d, 1).astype(BF16)
        go(back_copy(d))

    def take(d):
        keep[d] = backward(d, 0)
        back_copy(d).wait_recv()
        keep[d] += back_in[d].astype(F32)

    def near_copy(way, part):
        d = 4 if part == 2 else (3 if way == 0 else 5)
        step = 2 if part == 2 else 1
        span = pl.ds((part if part < 2 else way) * HALF, HALF)
        return remote(
            near_out.at[way, step - 1, span], near_in.at[way, step - 1, span],
            near_send.at[way, part], near_recv.at[way, part], at(dz=RING - step if way == 0 else step),
        )

    def root_copy(d, chunk, from_lane):
        span = pl.ds(chunk * HALF, HALF) if d in (2, 6) else pl.ds(0, ROWS)
        return remote(
            root_out.at[DIRECT[d], span], root_in.at[from_lane, DIRECT[d], span],
            root_send.at[DIRECT[d], chunk], root_recv.at[from_lane, DIRECT[d], chunk],
            at(dz=RING - d, dx=from_lane, dc=from_lane),
        )

    halves = [slice(0, HALF), slice(HALF, ROWS)]
    for d in (4, 3, 5):
        give(d)
    take(4)
    for way in range(2):
        near_out[way, 1, halves[way]] = keep[4, halves[way]].astype(BF16)
        go(near_copy(way, 2))
    for way in range(2):
        take(3 if way == 0 else 5)
        near_out[way, 0] = keep[3 if way == 0 else 5].astype(BF16)
        go(near_copy(way, way))
        go(near_copy(way, 1 - way))
    for d in (1, 7, 0, 2, 6):
        give(d)

    for df in range(1, SIDE):
        g1_copy(df).wait_recv()
    g2_out[...] = jnp.sum(g1[...].astype(F32), axis=0)

    def g2_copy(dz):
        rows = pl.ds(pl.multiple_of(((z + dz) % RING) * 8, 8), 8)
        return remote(g2_out.at[rows], g2.at[z], g2_send.at[dz], g2_recv.at[dz], at(dz=dz))

    for dz in range(1, RING):
        go(g2_copy(dz))
    g2[z] = g2_out[pl.ds(pl.multiple_of(z * 8, 8), 8)]

    for d in (1, 7):
        take(d)
        root_out[DIRECT[d]] = keep[d].astype(BF16)
        go(root_copy(d, 0, lane))
    take(0)

    @pl.when(lane == 1)
    def _():
        root_out[DIRECT[0]] = keep[0].astype(BF16)
        root_copy(0, 0, lane).start()

    take(2)
    take(6)

    for i in range(2):
        for way in range(2):
            chunk, d = i ^ way, 2 if way == 0 else 6
            value = keep[d, halves[chunk]]
            near_copy(way, chunk).wait_recv()
            value = value + near_in[way, 0, halves[chunk]].astype(F32)
            if i == 0:
                near_copy(way, 2).wait_recv()
                value = value + near_in[way, 1, halves[chunk]].astype(F32)
            root_out[DIRECT[d], halves[chunk]] = value.astype(BF16)
            go(root_copy(d, chunk, lane))

    for dz in range(1, RING):
        g2_copy(dz).wait_recv()
    g3_out[...] = jnp.sum(g2[...], axis=0)

    def g3_copy(i):
        return remote(
            g3_out, g3.at[r * 4 + xh * 2 + c], g3_send.at[i], g3_recv.at[i],
            at(dx=i // 4, dc=(i // 2) % 2, dr=i % 2),
        )

    for i in range(1, 8):
        go(g3_copy(i))
    g3[r * 4 + xh * 2 + c] = g3_out[...]

    def fin_copy(chunk):
        span = pl.ds(chunk * HALF, HALF)
        return remote(done.at[span], igrad.at[span], fin_send.at[chunk], fin_recv.at[chunk], at(dr=1))

    own_igrad = pltpu.make_async_copy(done, igrad, local_sem.at[8])

    @pl.when(lane == 0)
    def _():
        for from_lane in range(2):
            for d in (1, 7, 0) if from_lane else (1, 7):
                root_copy(d, 0, from_lane).wait_recv()
        for chunk in range(2):
            value = keep[0, halves[chunk]]
            for from_lane in range(2):
                for d in (1, 7, 0) if from_lane else (1, 7):
                    value = value + root_in[from_lane, DIRECT[d], halves[chunk]].astype(F32)
            for from_lane in range(2):
                for d in (2, 6):
                    root_copy(d, chunk, from_lane).wait_recv()
                    value = value + root_in[from_lane, DIRECT[d], halves[chunk]].astype(F32)
            done[halves[chunk]] = value.astype(BF16)
            fin_copy(chunk).start()
        own_igrad.start()

    for i in range(1, 8):
        g3_copy(i).wait_recv()
    scale = float(NODES * PARTS) ** -0.5
    for half in range(2):
        four = (g3[4 * half] + g3[4 * half + 1]) + (g3[4 * half + 2] + g3[4 * half + 3])
        g4_out[:, half * TILE:(half + 1) * TILE] = four * scale
    own_rows = pl.ds(pl.multiple_of(z * 8, 8), 8)

    def g4_copy(dz):
        return remote(g4_out, wgrad.at[own_rows], g4_send.at[dz], g4_recv.at[dz], at(dz=dz))

    for dz in range(1, RING):
        go(g4_copy(dz))
    own_wgrad = pltpu.make_async_copy(g4_out, wgrad.at[own_rows], local_sem.at[7])
    own_wgrad.start()

    @pl.when(lane == 1)
    def _():
        for chunk in range(2):
            fin_copy(chunk).wait_recv()

    @pl.when(lane == 0)
    def _():
        for first in firsts:
            first_copy(*first).wait_send()
        for chunk in range(2):
            fin_copy(chunk).wait_send()
        own_igrad.wait()

    @pl.when(lane == 1)
    def _():
        root_copy(0, 0, lane).wait_send()

    for copy in pending:
        copy.wait_send()
    for df in range(1, SIDE):
        hid_copy(df).wait_recv()
    for dz in range(1, RING):
        g4_copy(dz).wait_recv()
    own_hid.wait()
    own_wgrad.wait()


def hand_over(hid, wgrad, igrad, hid_to, wgrad_to, igrad_to):
    hid_to[...] = hid[...]
    wgrad_to[...] = wgrad[...]
    igrad_to[...] = igrad[...]


def body(features_t, tile_values, tile_rows, tile_cols, tile_count, weight, cotangent_t):
    anywhere = pl.BlockSpec(memory_space=pl.ANY)
    vmem, dma = pltpu.VMEM, pltpu.SemaphoreType.DMA
    block = (SIDE, ROWS, TILE)
    panel = (ROWS, NODES)
    out_shape = (
        jax.ShapeDtypeStruct((ROWS, NODES), BF16),
        jax.ShapeDtypeStruct((ROWS, 256), F32),
        jax.ShapeDtypeStruct((ROWS, NODES), BF16),
    )
    results = pl.pallas_call(
        kernel,
        out_shape=out_shape,
        in_specs=[anywhere] * 7,
        out_specs=(anywhere, anywhere, anywhere),
        scratch_shapes=[
            pltpu.SMEM((SLOTS, 1, PARTS), jnp.int32),
            pltpu.SMEM((SLOTS, 1, PARTS), jnp.int32),
            pltpu.SMEM((1, PARTS), jnp.int32),
            vmem((16, SLOTS, TILE, TILE), BF16),
            vmem((SLOTS + 1, TILE, TILE), BF16),
            vmem((16, NODES, NODES), BF16),
            vmem((RING, 2, *panel), BF16),
            vmem(panel, F32),
            vmem((SIDE, ROWS, 256), BF16),
            vmem((256, 256), BF16),
            vmem(block, BF16),
            vmem(block, BF16),
            vmem((2, *block), BF16),
            vmem(block, BF16),
            vmem(block, BF16),
            vmem(block, BF16),
            vmem(block, BF16),
            vmem(block, BF16),
            vmem((ROWS, TILE), F32),
            vmem((RING, 8, TILE), F32),
            vmem((8, TILE), F32),
            vmem((8, 8, TILE), F32),
            vmem((8, 256), F32),
            vmem((RING, *panel), BF16),
            vmem((RING, *panel), BF16),
            vmem((RING, *panel), F32),
            vmem((2, 2, *panel), BF16),
            vmem((2, 2, *panel), BF16),
            vmem((5, *panel), BF16),
            vmem((2, 5, *panel), BF16),
            vmem(panel, BF16),
            dma((16,)), dma((9,)), dma((2, 5, 2)), dma((5, 2)), dma((2, 3)), dma((2, 3)), dma((RING,)), dma((RING,)),
            dma((SIDE,)), dma((SIDE,)), dma((SIDE,)), dma((SIDE,)),
            dma((2, SIDE)), dma((2, SIDE)), dma((SIDE,)), dma((SIDE,)),
            dma((SIDE,)), dma((SIDE,)), dma((SIDE,)), dma((SIDE,)),
            dma((RING,)), dma((RING,)), dma((8,)), dma((8,)), dma((RING,)), dma((RING,)),
            dma((RING,)), dma((RING,)), dma((2, 3)), dma((2, 3)), dma((5, 2)), dma((2, 5, 2)), dma((2,)), dma((2,)),
        ],
        compiler_params=pltpu.CompilerParams(
            collective_id=0, has_side_effects=True, vmem_limit_bytes=VMEM_BYTES
        ),
    )(
        features_t, tile_values, jnp.transpose(tile_rows, (2, 0, 1)), jnp.transpose(tile_cols, (2, 0, 1)),
        tile_count, weight, cotangent_t,
    )
    return pl.pallas_call(
        hand_over,
        out_shape=out_shape,
        in_specs=[pl.BlockSpec(memory_space=vmem)] * 3,
        out_specs=(pl.BlockSpec(memory_space=vmem),) * 3,
    )(*results)


def solution(mesh):
    return jax.shard_map(
        body,
        mesh=mesh,
        in_specs=(
            P("feat", "blk"),
            P("blk", None, None, None, None),
            P("blk", None, None),
            P("blk", None, None),
            P("blk", None),
            P("feat", None),
            P("feat", "blk"),
        ),
        out_specs=(P("feat", "blk"), P("feat", None), P("feat", "blk")),
        check_vma=False,
    )
```

```python
import jax
import jax.numpy as jnp
from jax import lax
from jax.experimental import pallas as pl
from jax.experimental.pallas import tpu as pltpu
from jax.sharding import PartitionSpec as P

MESH = pl.DeviceIdType.MESH
BF16, F32 = jnp.bfloat16, jnp.float32
RING = 8
SIDE = 4
SLOTS = 12
TILE = 128
ROWS = 64
NODES = 512
PARTS = 32
HALF = ROWS // 2
VMEM_BYTES = 62 * 1024 * 1024

ORDER = [(d, cc) for d in (0, 1, 7, 2, 6, 3, 5, 4) for cc in (0, 1)]
PLACE = {pair: n for n, pair in enumerate(ORDER)}
DIRECT = {2: 0, 6: 1, 1: 2, 7: 3, 0: 4}


def kernel(
    feat, tiles, rows_hbm, cols_hbm, count_hbm, weight, cot,
    hid, wgrad, igrad,
    tile_rows, tile_cols, tile_count,
    raw, acc, dense, panels, agg, w_all, w_turned, cot_all,
    agg_out, agg_in, hid_out, sig_out, sig_in,
    g1_out, g1, g2_out, g2, g3_out, g3, g4_out,
    back_out, back_in, keep, near_out, near_in, root_out, root_in, fin_out, fin_in, done,
    tile_sem, local_sem, first_send, first_recv, second_send, second_recv, core_send, core_recv,
    w_send, w_recv, cot_send, cot_recv, agg_send, agg_recv, sig_send, sig_recv,
    hid_send, hid_recv, g1_send, g1_recv, g2_send, g2_recv, g3_send, g3_recv, g4_send, g4_recv,
    back_send, back_recv, near_send, near_recv, root_send, root_recv, fin_send, fin_recv,
):
    p, r, f = lax.axis_index("blk"), lax.axis_index("rep"), lax.axis_index("feat")
    z, xh, c = p // 4, (p // 2) % 2, p % 2
    lane = (c + r) % 2

    def at(dz=0, dx=0, dc=0, dr=0, df=0):
        nz = (z + dz) % RING
        nx, nc, nr = (xh + dx) % 2, (c + dc) % 2, (r + dr) % 2
        return (nz * 4 + nx * 2 + nc, nr, (f + df) % SIDE)

    pending = []

    def go(copy):
        copy.start()
        pending.append(copy)

    def remote(src, dst, send, recv, device):
        return pltpu.make_async_remote_copy(
            src_ref=src, dst_ref=dst, send_sem=send, recv_sem=recv, device_id=device, device_id_type=MESH
        )

    partners = [at(dz=dz) for dz in (4, 3, 5, 2, 6, 1, 7)]
    partners += [at(dz=dz, dx=1, dc=1, dr=1) for dz in (2, 6, 1, 7, 0)]
    partners += [at(dr=dr, df=df) for df in (2, 1, 3, 0) for dr in range(2) if dr or df]
    partners += [at(dc=1), at(dx=1), at(dx=1, dr=1), at(dc=1, dr=1), at(dx=1, dc=1)]
    barrier = pltpu.get_barrier_semaphore()
    for device in partners:
        pl.semaphore_signal(barrier, inc=1, device_id=device, device_id_type=MESH)

    def tile_copy(n):
        half = n // 2
        odd, step = half % 2, (half + 1) // 2
        d = (odd * step + (1 - odd) * (RING - step)) % RING
        source = ((z + RING - d) % RING) * 4 + ((xh + lane + n % 2) % 2) * 2 + r
        section = (p + PARTS - source) % PARTS
        return section, pltpu.make_async_copy(tiles.at[0, section], raw.at[n], tile_sem.at[n])

    own_feat = pltpu.make_async_copy(feat, panels.at[0, 0], local_sem.at[0])
    own_w = pltpu.make_async_copy(weight, w_all.at[f], local_sem.at[1])
    own_lanes = pl.ds(pl.multiple_of(f * TILE, TILE), TILE)
    own_cot = pltpu.make_async_copy(cot.at[:, own_lanes], cot_all.at[f], local_sem.at[2])

    scalar_copies = [
        pltpu.make_async_copy(src, dst, local_sem.at[3 + i])
        for i, (src, dst) in enumerate(((rows_hbm, tile_rows), (cols_hbm, tile_cols), (count_hbm, tile_count)))
    ]
    for copy in scalar_copies:
        copy.start()

    @pl.when(lane == 0)
    def _():
        own_feat.start()

    own_w.start()
    own_cot.start()

    def start_tiles(n, carried):
        tile_copy(n)[1].start()
        return carried

    lax.fori_loop(0, 16, start_tiles, 0)

    acc[SLOTS] = jnp.zeros((TILE, TILE), BF16)
    agg[...] = jnp.zeros_like(agg)
    pl.semaphore_wait(barrier, len(partners))

    def home(dz):
        return at(dz=dz, dx=lane, dc=lane, dr=lane)

    def first_copy(d, chunk):
        span = pl.ds(chunk * HALF, HALF) if d in (2, 6) else pl.ds(0, ROWS)
        return remote(
            feat.at[span], panels.at[d, 0, span],
            first_send.at[DIRECT[d], chunk], first_recv.at[DIRECT[d], chunk], home(d),
        )

    for i in range(2):
        for d in (2, 6):
            go(first_copy(d, i ^ (d == 6)))
    for d in (1, 7):
        go(first_copy(d, 0))

    @pl.when(lane == 1)
    def _():
        first_copy(0, 0).start()

    def second_copy(way, part):
        d = 2 if way == 0 else RING - 2
        step = 2 if part == 2 else 1
        to = d + step if way == 0 else d - step
        chunk = part if part < 2 else way
        span = pl.ds(chunk * HALF, HALF)
        return remote(
            panels.at[d, 0, span], panels.at[to, 0, span],
            second_send.at[way, part], second_recv.at[way, part], at(dz=step if way == 0 else RING - step),
        )

    def core_copy(d):
        return remote(panels.at[d, 0], panels.at[d, 1], core_send.at[d], core_recv.at[d], at(dc=1))

    def w_copy(df):
        return remote(weight, w_all.at[f], w_send.at[df], w_recv.at[df], at(df=df))

    def cot_copy(df):
        lanes = pl.ds(pl.multiple_of(((f + df) % SIDE) * TILE, TILE), TILE)
        return remote(cot.at[:, lanes], cot_all.at[f], cot_send.at[df], cot_recv.at[df], at(df=df))

    for df in range(1, SIDE):
        go(w_copy(df))
        go(cot_copy(df))

    def densify(n, carried):
        section, copy = tile_copy(n)
        copy.wait()
        live = tile_count[0, section]
        target = [
            jnp.where(t < live, tile_rows[t, 0, section] * SIDE + tile_cols[t, 0, section], 16)
            for t in range(SLOTS)
        ]
        for t in range(SLOTS):
            before = jnp.int32(SLOTS)
            for u in range(t):
                before = jnp.where(target[u] == target[t], u, before)
            acc[t] = raw[n, t] + acc[before]
        for b in range(16):
            last = jnp.int32(SLOTS)
            for t in range(SLOTS):
                last = jnp.where(target[t] == b, t, last)
            i, j = b // SIDE, b % SIDE
            dense[n, i * TILE:(i + 1) * TILE, j * TILE:(j + 1) * TILE] = acc[last]
        return carried

    def forward(d, cc):
        if cc:
            core_copy(d).wait_recv()
        agg[...] += lax.dot_general(
            panels[d, cc], dense[PLACE[d, cc]], (((1,), (1,)), ((), ())), preferred_element_type=F32
        )

    for copy in scalar_copies:
        copy.wait()
    lax.fori_loop(0, 16, densify, 0)
    for i in range(2):
        for way in range(2):
            chunk = i ^ way
            first_copy(2 if way == 0 else 6, chunk).wait_recv()
            if i == 0:
                go(second_copy(way, 2))
            go(second_copy(way, chunk))
    go(core_copy(2))
    go(core_copy(6))
    for d in (1, 7):
        first_copy(d, 0).wait_recv()
        go(core_copy(d))

    @pl.when(lane == 0)
    def _():
        own_feat.wait()

    @pl.when(lane == 1)
    def _():
        first_copy(0, 0).wait_recv()

    go(core_copy(0))
    for d in (2, 6, 1, 7, 0):
        forward(d, 0)
        forward(d, 1)
    own_w.wait()
    for df in range(1, SIDE):
        w_copy(df).wait_recv()
    w_turned[...] = w_all[...].reshape(256, 256).astype(F32).T.astype(BF16)
    for way in range(2):
        second_copy(way, 0).wait_recv()
        second_copy(way, 1).wait_recv()
        go(core_copy(3 if way == 0 else 5))
    for way in range(2):
        second_copy(way, 2).wait_recv()
    go(core_copy(4))
    for d in (3, 5, 4):
        forward(d, 0)
    for d in (3, 5, 4):
        forward(d, 1)

    def agg_copy(dr, df):
        return remote(
            agg_out.at[(f + df) % SIDE], agg_in.at[r, f], agg_send.at[dr, df], agg_recv.at[dr, df], at(dr=dr, df=df)
        )

    group = [(dr, df) for df in (2, 1, 3, 0) for dr in (1, 0) if dr or df]
    for b in range(SIDE):
        agg_out[b] = agg[:, b * TILE:(b + 1) * TILE].astype(BF16)
    for dr, df in group:
        go(agg_copy(dr, df))
    agg_in[r, f] = agg_out[f]
    own_cot.wait()
    for df in range(1, SIDE):
        cot_copy(df).wait_recv()
    for dr, df in group:
        agg_copy(dr, df).wait_recv()
    summed = (agg_in[0].astype(F32) + agg_in[1].astype(F32)).reshape(256, TILE).astype(BF16)
    pre_act = jnp.dot(w_turned[...], summed, preferred_element_type=F32)
    gate = 1.0 / (1.0 + jnp.exp(-pre_act))
    grad = cot_all[...].reshape(256, TILE).astype(F32)
    pre_grad = (grad * gate * (1.0 + pre_act * (1.0 - gate))).astype(BF16)
    signal = jnp.dot(w_all[...].reshape(256, 256), pre_grad, preferred_element_type=F32)
    sig_out[...] = signal.astype(BF16).reshape(SIDE, ROWS, TILE)

    def sig_copy(df):
        return remote(sig_out.at[(f + df) % SIDE], sig_in.at[f], sig_send.at[df], sig_recv.at[df], at(df=df))

    for df in (2, 1, 3):
        go(sig_copy(df))
    sig_in[f] = sig_out[f]

    grad_rows = jnp.where(r == 0, pre_grad[:TILE].astype(F32), pre_grad[TILE:].astype(F32)).astype(BF16)
    share = lax.dot_general(summed, grad_rows, (((1,), (1,)), ((), ())), preferred_element_type=F32)
    g1_out[...] = share.astype(BF16).reshape(SIDE, ROWS, TILE)

    def g1_copy(df):
        return remote(g1_out.at[(f + df) % SIDE], g1.at[f], g1_send.at[df], g1_recv.at[df], at(df=df))

    for df in range(1, SIDE):
        go(g1_copy(df))
    g1[f] = g1_out[f]

    hid_out[...] = (pre_act * gate).astype(BF16).reshape(SIDE, ROWS, TILE)

    def hid_copy(df):
        return remote(
            hid_out.at[(f + df) % SIDE], hid.at[:, own_lanes], hid_send.at[df], hid_recv.at[df], at(df=df)
        )

    own_hid = pltpu.make_async_copy(hid_out.at[f], hid.at[:, own_lanes], local_sem.at[6])
    own_hid.start()
    for df in range(1, SIDE):
        go(hid_copy(df))

    for df in (2, 1, 3):
        sig_copy(df).wait_recv()
    signal_row = jnp.concatenate([sig_in[b] for b in range(SIDE)], axis=1)

    def backward(d, cc):
        return jnp.dot(signal_row, dense[PLACE[d, cc]], preferred_element_type=F32)

    def back_copy(d):
        return remote(back_out.at[d], back_in.at[d], back_send.at[d], back_recv.at[d], at(dc=1))

    def give(d):
        back_out[d] = backward(d, 1).astype(BF16)
        go(back_copy(d))

    def take(d):
        keep[d] = backward(d, 0)
        back_copy(d).wait_recv()
        keep[d] += back_in[d].astype(F32)

    def near_copy(way, part):
        d = 4 if part == 2 else (3 if way == 0 else 5)
        step = 2 if part == 2 else 1
        span = pl.ds((part if part < 2 else way) * HALF, HALF)
        return remote(
            near_out.at[way, step - 1, span], near_in.at[way, step - 1, span],
            near_send.at[way, part], near_recv.at[way, part], at(dz=RING - step if way == 0 else step),
        )

    def root_copy(d, chunk):
        span = pl.ds(chunk * HALF, HALF) if d in (2, 6) else pl.ds(0, ROWS)
        return remote(
            root_out.at[DIRECT[d], span], root_in.at[DIRECT[d], span],
            root_send.at[DIRECT[d], chunk], root_recv.at[DIRECT[d], chunk], home(RING - d),
        )

    halves = [slice(0, HALF), slice(HALF, ROWS)]
    for d in (4, 3, 5):
        give(d)
    take(4)
    for way in range(2):
        near_out[way, 1, halves[way]] = keep[4, halves[way]].astype(BF16)
        go(near_copy(way, 2))
    for df in range(1, SIDE):
        g1_copy(df).wait_recv()
    g2_out[...] = jnp.sum(g1[...].astype(F32), axis=0)

    def g2_copy(dz):
        rows = pl.ds(pl.multiple_of(((z + dz) % RING) * 8, 8), 8)
        return remote(g2_out.at[rows], g2.at[z], g2_send.at[dz], g2_recv.at[dz], at(dz=dz))

    for dz in range(1, RING):
        go(g2_copy(dz))
    g2[z] = g2_out[pl.ds(pl.multiple_of(z * 8, 8), 8)]

    for way in range(2):
        take(3 if way == 0 else 5)
        near_out[way, 0] = keep[3 if way == 0 else 5].astype(BF16)
        go(near_copy(way, way))
        go(near_copy(way, 1 - way))
    for d in (1, 7, 0, 2, 6):
        give(d)

    for d in (1, 7):
        take(d)
        root_out[DIRECT[d]] = keep[d].astype(BF16)
        go(root_copy(d, 0))
    take(0)

    @pl.when(lane == 1)
    def _():
        root_out[DIRECT[0]] = keep[0].astype(BF16)
        root_copy(0, 0).start()

    take(2)
    take(6)

    for dz in range(1, RING):
        g2_copy(dz).wait_recv()
    g3_out[...] = jnp.sum(g2[...], axis=0)

    def g3_copy(i):
        return remote(
            g3_out, g3.at[r * 4 + xh * 2 + c], g3_send.at[i], g3_recv.at[i],
            at(dx=i // 4, dc=(i // 2) % 2, dr=i % 2),
        )

    for i in range(1, 8):
        go(g3_copy(i))
    g3[r * 4 + xh * 2 + c] = g3_out[...]

    for i in range(2):
        for way in range(2):
            chunk, d = i ^ way, 2 if way == 0 else 6
            value = keep[d, halves[chunk]]
            near_copy(way, chunk).wait_recv()
            value = value + near_in[way, 0, halves[chunk]].astype(F32)
            if i == 0:
                near_copy(way, 2).wait_recv()
                value = value + near_in[way, 1, halves[chunk]].astype(F32)
            root_out[DIRECT[d], halves[chunk]] = value.astype(BF16)
            go(root_copy(d, chunk))

    for i in range(1, 8):
        g3_copy(i).wait_recv()
    scale = float(NODES * PARTS) ** -0.5
    for half in range(2):
        four = (g3[4 * half] + g3[4 * half + 1]) + (g3[4 * half + 2] + g3[4 * half + 3])
        g4_out[:, half * TILE:(half + 1) * TILE] = four * scale
    own_rows = pl.ds(pl.multiple_of(z * 8, 8), 8)

    def g4_copy(dz):
        return remote(g4_out, wgrad.at[own_rows], g4_send.at[dz], g4_recv.at[dz], at(dz=dz))

    for dz in range(1, RING):
        go(g4_copy(dz))
    own_wgrad = pltpu.make_async_copy(g4_out, wgrad.at[own_rows], local_sem.at[7])
    own_wgrad.start()

    def fin_copy(chunk):
        span = pl.ds(chunk * HALF, HALF)
        return remote(fin_out.at[span], fin_in.at[span], fin_send.at[chunk], fin_recv.at[chunk], at(dr=1))

    @pl.when(lane == 0)
    def _():
        root_in[DIRECT[0]] = keep[0].astype(BF16)

    @pl.when(lane == 1)
    def _():
        root_copy(0, 0).wait_recv()

    for d in (1, 7):
        root_copy(d, 0).wait_recv()
    for chunk in range(2):
        value = root_in[DIRECT[0], halves[chunk]].astype(F32)
        for d in (1, 7, 2, 6):
            if d in (2, 6):
                root_copy(d, chunk).wait_recv()
            value = value + root_in[DIRECT[d], halves[chunk]].astype(F32)
        fin_out[halves[chunk]] = value.astype(BF16)
        go(fin_copy(chunk))

    for chunk in range(2):
        fin_copy(chunk).wait_recv()
    done[...] = (fin_out[...].astype(F32) + fin_in[...].astype(F32)).astype(BF16)
    own_igrad = pltpu.make_async_copy(done, igrad, local_sem.at[8])
    own_igrad.start()

    @pl.when(lane == 1)
    def _():
        first_copy(0, 0).wait_send()
        root_copy(0, 0).wait_send()

    for copy in pending:
        copy.wait_send()
    for df in range(1, SIDE):
        hid_copy(df).wait_recv()
    for dz in range(1, RING):
        g4_copy(dz).wait_recv()
    own_hid.wait()
    own_wgrad.wait()
    own_igrad.wait()


def hand_over(hid, wgrad, igrad, hid_to, wgrad_to, igrad_to):
    hid_to[...] = hid[...]
    wgrad_to[...] = wgrad[...]
    igrad_to[...] = igrad[...]


def body(features_t, tile_values, tile_rows, tile_cols, tile_count, weight, cotangent_t):
    anywhere = pl.BlockSpec(memory_space=pl.ANY)
    vmem, dma = pltpu.VMEM, pltpu.SemaphoreType.DMA
    block = (SIDE, ROWS, TILE)
    panel = (ROWS, NODES)
    out_shape = (
        jax.ShapeDtypeStruct((ROWS, NODES), BF16),
        jax.ShapeDtypeStruct((ROWS, 256), F32),
        jax.ShapeDtypeStruct((ROWS, NODES), BF16),
    )
    results = pl.pallas_call(
        kernel,
        out_shape=out_shape,
        in_specs=[anywhere] * 7,
        out_specs=(anywhere, anywhere, anywhere),
        scratch_shapes=[
            pltpu.SMEM((SLOTS, 1, PARTS), jnp.int32),
            pltpu.SMEM((SLOTS, 1, PARTS), jnp.int32),
            pltpu.SMEM((1, PARTS), jnp.int32),
            vmem((16, SLOTS, TILE, TILE), BF16),
            vmem((SLOTS + 1, TILE, TILE), BF16),
            vmem((16, NODES, NODES), BF16),
            vmem((RING, 2, *panel), BF16),
            vmem(panel, F32),
            vmem((SIDE, ROWS, 256), BF16),
            vmem((256, 256), BF16),
            vmem(block, BF16),
            vmem(block, BF16),
            vmem((2, *block), BF16),
            vmem(block, BF16),
            vmem(block, BF16),
            vmem(block, BF16),
            vmem(block, BF16),
            vmem(block, BF16),
            vmem((ROWS, TILE), F32),
            vmem((RING, 8, TILE), F32),
            vmem((8, TILE), F32),
            vmem((8, 8, TILE), F32),
            vmem((8, 256), F32),
            vmem((RING, *panel), BF16),
            vmem((RING, *panel), BF16),
            vmem((RING, *panel), F32),
            vmem((2, 2, *panel), BF16),
            vmem((2, 2, *panel), BF16),
            vmem((5, *panel), BF16),
            vmem((5, *panel), BF16),
            vmem(panel, BF16),
            vmem(panel, BF16),
            vmem(panel, BF16),
            dma((16,)), dma((9,)), dma((5, 2)), dma((5, 2)), dma((2, 3)), dma((2, 3)), dma((RING,)), dma((RING,)),
            dma((SIDE,)), dma((SIDE,)), dma((SIDE,)), dma((SIDE,)),
            dma((2, SIDE)), dma((2, SIDE)), dma((SIDE,)), dma((SIDE,)),
            dma((SIDE,)), dma((SIDE,)), dma((SIDE,)), dma((SIDE,)),
            dma((RING,)), dma((RING,)), dma((8,)), dma((8,)), dma((RING,)), dma((RING,)),
            dma((RING,)), dma((RING,)), dma((2, 3)), dma((2, 3)), dma((5, 2)), dma((5, 2)), dma((2,)), dma((2,)),
        ],
        compiler_params=pltpu.CompilerParams(
            collective_id=0, has_side_effects=True, vmem_limit_bytes=VMEM_BYTES
        ),
    )(
        features_t, tile_values, jnp.transpose(tile_rows, (2, 0, 1)), jnp.transpose(tile_cols, (2, 0, 1)),
        tile_count, weight, cotangent_t,
    )
    return pl.pallas_call(
        hand_over,
        out_shape=out_shape,
        in_specs=[pl.BlockSpec(memory_space=vmem)] * 3,
        out_specs=(pl.BlockSpec(memory_space=vmem),) * 3,
    )(*results)


def solution(mesh):
    return jax.shard_map(
        body,
        mesh=mesh,
        in_specs=(
            P("feat", "blk"),
            P("blk", None, None, None, None),
            P("blk", None, None),
            P("blk", None, None),
            P("blk", None),
            P("feat", None),
            P("feat", "blk"),
        ),
        out_specs=(P("feat", "blk"), P("feat", None), P("feat", "blk")),
        check_vma=False,
    )
```

```python
import jax
import jax.numpy as jnp
from jax import lax
from jax.experimental import pallas as pl
from jax.experimental.pallas import tpu as pltpu
from jax.sharding import PartitionSpec as P

MESH = pl.DeviceIdType.MESH
BF16, F32 = jnp.bfloat16, jnp.float32
RING = 8
SIDE = 4
SLOTS = 12
TILE = 128
ROWS = 64
NODES = 512
PARTS = 32
HALF = ROWS // 2
VMEM_BYTES = 62 * 1024 * 1024

ORDER = [(d, cc) for d in (0, 1, 7, 2, 6, 3, 5, 4) for cc in (0, 1)]
PLACE = {pair: n for n, pair in enumerate(ORDER)}
DIRECT = {2: 0, 6: 1, 1: 2, 7: 3, 0: 4}


def kernel(
    feat, tiles, rows_hbm, cols_hbm, count_hbm, weight, cot,
    hid, wgrad, fin_own, fin_other,
    tile_rows, tile_cols, tile_count,
    raw, acc, dense, panels, agg, w_all, w_turned, cot_all,
    agg_out, agg_in, hid_out, sig_out, sig_in,
    g1_out, g1, g2_out, g2, g3_out, g3, g4_out,
    back_out, back_in, keep, near_out, near_in, root_out, root_in, fin_out,
    tile_sem, local_sem, first_send, first_recv, second_send, second_recv, core_send, core_recv,
    w_send, w_recv, cot_send, cot_recv, agg_send, agg_recv, sig_send, sig_recv,
    hid_send, hid_recv, g1_send, g1_recv, g2_send, g2_recv, g3_send, g3_recv, g4_send, g4_recv,
    back_send, back_recv, near_send, near_recv, root_send, root_recv, fin_send, fin_recv,
):
    p, r, f = lax.axis_index("blk"), lax.axis_index("rep"), lax.axis_index("feat")
    z, xh, c = p // 4, (p // 2) % 2, p % 2
    lane = (c + r) % 2

    def at(dz=0, dx=0, dc=0, dr=0, df=0):
        nz = (z + dz) % RING
        nx, nc, nr = (xh + dx) % 2, (c + dc) % 2, (r + dr) % 2
        return (nz * 4 + nx * 2 + nc, nr, (f + df) % SIDE)

    pending = []

    def go(copy):
        copy.start()
        pending.append(copy)

    def remote(src, dst, send, recv, device):
        return pltpu.make_async_remote_copy(
            src_ref=src, dst_ref=dst, send_sem=send, recv_sem=recv, device_id=device, device_id_type=MESH
        )

    partners = [at(dz=dz) for dz in (4, 3, 5, 2, 6, 1, 7)]
    partners += [at(dz=dz, dx=1, dc=1, dr=1) for dz in (2, 6, 1, 7, 0)]
    partners += [at(dr=dr, df=df) for df in (2, 1, 3, 0) for dr in range(2) if dr or df]
    partners += [at(dc=1), at(dx=1), at(dx=1, dr=1), at(dc=1, dr=1), at(dx=1, dc=1)]
    barrier = pltpu.get_barrier_semaphore()
    for device in partners:
        pl.semaphore_signal(barrier, inc=1, device_id=device, device_id_type=MESH)

    def tile_copy(n):
        half = n // 2
        odd, step = half % 2, (half + 1) // 2
        d = (odd * step + (1 - odd) * (RING - step)) % RING
        source = ((z + RING - d) % RING) * 4 + ((xh + lane + n % 2) % 2) * 2 + r
        section = (p + PARTS - source) % PARTS
        return section, pltpu.make_async_copy(tiles.at[0, section], raw.at[n], tile_sem.at[n])

    own_feat = pltpu.make_async_copy(feat, panels.at[0, 0], local_sem.at[0])
    own_w = pltpu.make_async_copy(weight, w_all.at[f], local_sem.at[1])
    own_lanes = pl.ds(pl.multiple_of(f * TILE, TILE), TILE)
    own_cot = pltpu.make_async_copy(cot.at[:, own_lanes], cot_all.at[f], local_sem.at[2])

    scalar_copies = [
        pltpu.make_async_copy(src, dst, local_sem.at[3 + i])
        for i, (src, dst) in enumerate(((rows_hbm, tile_rows), (cols_hbm, tile_cols), (count_hbm, tile_count)))
    ]
    for copy in scalar_copies:
        copy.start()

    @pl.when(lane == 0)
    def _():
        own_feat.start()

    own_w.start()
    own_cot.start()

    def start_tiles(n, carried):
        tile_copy(n)[1].start()
        return carried

    lax.fori_loop(0, 16, start_tiles, 0)

    acc[SLOTS] = jnp.zeros((TILE, TILE), BF16)
    agg[...] = jnp.zeros_like(agg)
    pl.semaphore_wait(barrier, len(partners))

    def home(dz):
        return at(dz=dz, dx=lane, dc=lane, dr=lane)

    def first_copy(d, chunk):
        span = pl.ds(chunk * HALF, HALF) if d in (2, 6) else pl.ds(0, ROWS)
        return remote(
            feat.at[span], panels.at[d, 0, span],
            first_send.at[DIRECT[d], chunk], first_recv.at[DIRECT[d], chunk], home(d),
        )

    for i in range(2):
        for d in (2, 6):
            go(first_copy(d, i ^ (d == 6)))
    for d in (1, 7):
        go(first_copy(d, 0))

    @pl.when(lane == 1)
    def _():
        first_copy(0, 0).start()

    def second_copy(way, part):
        d = 2 if way == 0 else RING - 2
        step = 2 if part == 2 else 1
        to = d + step if way == 0 else d - step
        chunk = part if part < 2 else way
        span = pl.ds(chunk * HALF, HALF)
        return remote(
            panels.at[d, 0, span], panels.at[to, 0, span],
            second_send.at[way, part], second_recv.at[way, part], at(dz=step if way == 0 else RING - step),
        )

    def core_copy(d):
        return remote(panels.at[d, 0], panels.at[d, 1], core_send.at[d], core_recv.at[d], at(dc=1))

    def w_copy(df):
        return remote(weight, w_all.at[f], w_send.at[df], w_recv.at[df], at(df=df))

    def cot_copy(df):
        lanes = pl.ds(pl.multiple_of(((f + df) % SIDE) * TILE, TILE), TILE)
        return remote(cot.at[:, lanes], cot_all.at[f], cot_send.at[df], cot_recv.at[df], at(df=df))

    for df in range(1, SIDE):
        go(w_copy(df))
        go(cot_copy(df))

    def densify(n, carried):
        section, copy = tile_copy(n)
        copy.wait()
        live = tile_count[0, section]
        target = [
            jnp.where(t < live, tile_rows[t, 0, section] * SIDE + tile_cols[t, 0, section], 16)
            for t in range(SLOTS)
        ]
        for t in range(SLOTS):
            before = jnp.int32(SLOTS)
            for u in range(t):
                before = jnp.where(target[u] == target[t], u, before)
            acc[t] = raw[n, t] + acc[before]
        for b in range(16):
            last = jnp.int32(SLOTS)
            for t in range(SLOTS):
                last = jnp.where(target[t] == b, t, last)
            i, j = b // SIDE, b % SIDE
            dense[n, i * TILE:(i + 1) * TILE, j * TILE:(j + 1) * TILE] = acc[last]
        return carried

    def forward(d, cc):
        if cc:
            core_copy(d).wait_recv()
        agg[...] += lax.dot_general(
            panels[d, cc], dense[PLACE[d, cc]], (((1,), (1,)), ((), ())), preferred_element_type=F32
        )

    for copy in scalar_copies:
        copy.wait()
    lax.fori_loop(0, 16, densify, 0)
    for i in range(2):
        for way in range(2):
            chunk = i ^ way
            first_copy(2 if way == 0 else 6, chunk).wait_recv()
            if i == 0:
                go(second_copy(way, 2))
            go(second_copy(way, chunk))
    go(core_copy(2))
    go(core_copy(6))
    for d in (1, 7):
        first_copy(d, 0).wait_recv()
        go(core_copy(d))

    @pl.when(lane == 0)
    def _():
        own_feat.wait()

    @pl.when(lane == 1)
    def _():
        first_copy(0, 0).wait_recv()

    go(core_copy(0))
    for d in (2, 6, 1, 7, 0):
        forward(d, 0)
        forward(d, 1)
    own_w.wait()
    for df in range(1, SIDE):
        w_copy(df).wait_recv()
    w_turned[...] = w_all[...].reshape(256, 256).astype(F32).T.astype(BF16)
    for way in range(2):
        second_copy(way, 0).wait_recv()
        second_copy(way, 1).wait_recv()
        go(core_copy(3 if way == 0 else 5))
    forward(3, 0)
    for way in range(2):
        second_copy(way, 2).wait_recv()
    go(core_copy(4))
    forward(5, 0)
    forward(4, 0)
    for d in (3, 5, 4):
        forward(d, 1)

    def agg_copy(dr, df):
        return remote(
            agg_out.at[(f + df) % SIDE], agg_in.at[r, f], agg_send.at[dr, df], agg_recv.at[dr, df], at(dr=dr, df=df)
        )

    group = [(dr, df) for df in (2, 1, 3, 0) for dr in (1, 0) if dr or df]
    for b in range(SIDE):
        agg_out[b] = agg[:, b * TILE:(b + 1) * TILE].astype(BF16)
    for dr, df in group:
        go(agg_copy(dr, df))
    agg_in[r, f] = agg_out[f]
    own_cot.wait()
    for df in range(1, SIDE):
        cot_copy(df).wait_recv()
    for dr, df in group:
        agg_copy(dr, df).wait_recv()
    summed = (agg_in[0].astype(F32) + agg_in[1].astype(F32)).reshape(256, TILE).astype(BF16)
    pre_act = jnp.dot(w_turned[...], summed, preferred_element_type=F32)
    gate = 1.0 / (1.0 + jnp.exp(-pre_act))
    grad = cot_all[...].reshape(256, TILE).astype(F32)
    pre_grad = (grad * gate * (1.0 + pre_act * (1.0 - gate))).astype(BF16)
    signal = jnp.dot(w_all[...].reshape(256, 256), pre_grad, preferred_element_type=F32)
    sig_out[...] = signal.astype(BF16).reshape(SIDE, ROWS, TILE)

    def sig_copy(df):
        return remote(sig_out.at[(f + df) % SIDE], sig_in.at[f], sig_send.at[df], sig_recv.at[df], at(df=df))

    for df in (2, 1, 3):
        go(sig_copy(df))
    sig_in[f] = sig_out[f]

    grad_rows = jnp.where(r == 0, pre_grad[:TILE].astype(F32), pre_grad[TILE:].astype(F32)).astype(BF16)
    share = lax.dot_general(summed, grad_rows, (((1,), (1,)), ((), ())), preferred_element_type=F32)
    g1_out[...] = share.astype(BF16).reshape(SIDE, ROWS, TILE)

    def g1_copy(df):
        return remote(g1_out.at[(f + df) % SIDE], g1.at[f], g1_send.at[df], g1_recv.at[df], at(df=df))

    for df in range(1, SIDE):
        go(g1_copy(df))
    g1[f] = g1_out[f]

    hid_out[...] = (pre_act * gate).astype(BF16).reshape(SIDE, ROWS, TILE)

    def hid_copy(df):
        return remote(
            hid_out.at[(f + df) % SIDE], hid.at[:, own_lanes], hid_send.at[df], hid_recv.at[df], at(df=df)
        )

    own_hid = pltpu.make_async_copy(hid_out.at[f], hid.at[:, own_lanes], local_sem.at[6])
    own_hid.start()
    for df in range(1, SIDE):
        go(hid_copy(df))

    for df in (2, 1, 3):
        sig_copy(df).wait_recv()
    signal_row = jnp.concatenate([sig_in[b] for b in range(SIDE)], axis=1)

    def backward(d, cc):
        return jnp.dot(signal_row, dense[PLACE[d, cc]], preferred_element_type=F32)

    def back_copy(d):
        return remote(back_out.at[d], back_in.at[d], back_send.at[d], back_recv.at[d], at(dc=1))

    def give(d):
        back_out[d] = backward(d, 1).astype(BF16)
        go(back_copy(d))

    def take(d):
        keep[d] = backward(d, 0)
        back_copy(d).wait_recv()
        keep[d] += back_in[d].astype(F32)

    def near_copy(way, part):
        d = 4 if part == 2 else (3 if way == 0 else 5)
        step = 2 if part == 2 else 1
        span = pl.ds((part if part < 2 else way) * HALF, HALF)
        return remote(
            near_out.at[way, step - 1, span], near_in.at[way, step - 1, span],
            near_send.at[way, part], near_recv.at[way, part], at(dz=RING - step if way == 0 else step),
        )

    def root_copy(d, chunk):
        span = pl.ds(chunk * HALF, HALF) if d in (2, 6) else pl.ds(0, ROWS)
        return remote(
            root_out.at[DIRECT[d], span], root_in.at[DIRECT[d], span],
            root_send.at[DIRECT[d], chunk], root_recv.at[DIRECT[d], chunk], home(RING - d),
        )

    halves = [slice(0, HALF), slice(HALF, ROWS)]
    for d in (4, 3, 5):
        give(d)
    take(4)
    for way in range(2):
        near_out[way, 1, halves[way]] = keep[4, halves[way]].astype(BF16)
        go(near_copy(way, 2))
    for df in range(1, SIDE):
        g1_copy(df).wait_recv()
    g2_out[...] = jnp.sum(g1[...].astype(F32), axis=0)

    def g2_copy(dz):
        rows = pl.ds(pl.multiple_of(((z + dz) % RING) * 8, 8), 8)
        return remote(g2_out.at[rows], g2.at[z], g2_send.at[dz], g2_recv.at[dz], at(dz=dz))

    for dz in range(1, RING):
        go(g2_copy(dz))
    g2[z] = g2_out[pl.ds(pl.multiple_of(z * 8, 8), 8)]

    for way in range(2):
        take(3 if way == 0 else 5)
        near_out[way, 0] = keep[3 if way == 0 else 5].astype(BF16)
        go(near_copy(way, way))
        go(near_copy(way, 1 - way))
    for d in (1, 7, 0, 2, 6):
        give(d)

    for d in (1, 7):
        take(d)
        root_out[DIRECT[d]] = keep[d].astype(BF16)
        go(root_copy(d, 0))
    take(0)

    @pl.when(lane == 1)
    def _():
        root_out[DIRECT[0]] = keep[0].astype(BF16)
        root_copy(0, 0).start()

    take(2)
    take(6)

    for dz in range(1, RING):
        g2_copy(dz).wait_recv()
    g3_out[...] = jnp.sum(g2[...], axis=0)

    def g3_copy(i):
        return remote(
            g3_out, g3.at[r * 4 + xh * 2 + c], g3_send.at[i], g3_recv.at[i],
            at(dx=i // 4, dc=(i // 2) % 2, dr=i % 2),
        )

    for i in range(1, 8):
        go(g3_copy(i))
    g3[r * 4 + xh * 2 + c] = g3_out[...]

    for i in range(2):
        for way in range(2):
            chunk, d = i ^ way, 2 if way == 0 else 6
            value = keep[d, halves[chunk]]
            near_copy(way, chunk).wait_recv()
            value = value + near_in[way, 0, halves[chunk]].astype(F32)
            if i == 0:
                near_copy(way, 2).wait_recv()
                value = value + near_in[way, 1, halves[chunk]].astype(F32)
            root_out[DIRECT[d], halves[chunk]] = value.astype(BF16)
            go(root_copy(d, chunk))

    for i in range(1, 8):
        g3_copy(i).wait_recv()
    scale = float(NODES * PARTS) ** -0.5
    for half in range(2):
        four = (g3[4 * half] + g3[4 * half + 1]) + (g3[4 * half + 2] + g3[4 * half + 3])
        g4_out[:, half * TILE:(half + 1) * TILE] = four * scale
    own_rows = pl.ds(pl.multiple_of(z * 8, 8), 8)

    def g4_copy(dz):
        return remote(g4_out, wgrad.at[own_rows], g4_send.at[dz], g4_recv.at[dz], at(dz=dz))

    for dz in range(1, RING):
        go(g4_copy(dz))
    own_wgrad = pltpu.make_async_copy(g4_out, wgrad.at[own_rows], local_sem.at[7])
    own_wgrad.start()

    def fin_copy(chunk):
        span = pl.ds(chunk * HALF, HALF)
        return remote(fin_out.at[span], fin_other.at[span], fin_send.at[chunk], fin_recv.at[chunk], at(dr=1))

    @pl.when(lane == 0)
    def _():
        root_in[DIRECT[0]] = keep[0].astype(BF16)

    @pl.when(lane == 1)
    def _():
        root_copy(0, 0).wait_recv()

    for d in (1, 7):
        root_copy(d, 0).wait_recv()
    for chunk in range(2):
        value = root_in[DIRECT[0], halves[chunk]].astype(F32)
        for d in (1, 7, 2, 6):
            if d in (2, 6):
                root_copy(d, chunk).wait_recv()
            value = value + root_in[DIRECT[d], halves[chunk]].astype(F32)
        fin_out[halves[chunk]] = value.astype(BF16)
        go(fin_copy(chunk))
    own_fin = pltpu.make_async_copy(fin_out, fin_own, local_sem.at[8])
    own_fin.start()

    for chunk in range(2):
        fin_copy(chunk).wait_recv()

    @pl.when(lane == 1)
    def _():
        first_copy(0, 0).wait_send()
        root_copy(0, 0).wait_send()

    for copy in pending:
        copy.wait_send()
    for df in range(1, SIDE):
        hid_copy(df).wait_recv()
    for dz in range(1, RING):
        g4_copy(dz).wait_recv()
    own_hid.wait()
    own_wgrad.wait()
    own_fin.wait()


def hand_over(hid, wgrad, fin_own, fin_other, hid_to, wgrad_to, igrad_to):
    hid_to[...] = hid[...]
    wgrad_to[...] = wgrad[...]
    igrad_to[...] = (fin_own[...].astype(F32) + fin_other[...].astype(F32)).astype(BF16)


def body(features_t, tile_values, tile_rows, tile_cols, tile_count, weight, cotangent_t):
    anywhere = pl.BlockSpec(memory_space=pl.ANY)
    vmem, dma = pltpu.VMEM, pltpu.SemaphoreType.DMA
    block = (SIDE, ROWS, TILE)
    panel = (ROWS, NODES)
    out_shape = (
        jax.ShapeDtypeStruct((ROWS, NODES), BF16),
        jax.ShapeDtypeStruct((ROWS, 256), F32),
        jax.ShapeDtypeStruct((ROWS, NODES), BF16),
    )
    results = pl.pallas_call(
        kernel,
        out_shape=(*out_shape, out_shape[2]),
        in_specs=[anywhere] * 7,
        out_specs=(anywhere,) * 4,
        scratch_shapes=[
            pltpu.SMEM((SLOTS, 1, PARTS), jnp.int32),
            pltpu.SMEM((SLOTS, 1, PARTS), jnp.int32),
            pltpu.SMEM((1, PARTS), jnp.int32),
            vmem((16, SLOTS, TILE, TILE), BF16),
            vmem((SLOTS + 1, TILE, TILE), BF16),
            vmem((16, NODES, NODES), BF16),
            vmem((RING, 2, *panel), BF16),
            vmem(panel, F32),
            vmem((SIDE, ROWS, 256), BF16),
            vmem((256, 256), BF16),
            vmem(block, BF16),
            vmem(block, BF16),
            vmem((2, *block), BF16),
            vmem(block, BF16),
            vmem(block, BF16),
            vmem(block, BF16),
            vmem(block, BF16),
            vmem(block, BF16),
            vmem((ROWS, TILE), F32),
            vmem((RING, 8, TILE), F32),
            vmem((8, TILE), F32),
            vmem((8, 8, TILE), F32),
            vmem((8, 256), F32),
            vmem((RING, *panel), BF16),
            vmem((RING, *panel), BF16),
            vmem((RING, *panel), F32),
            vmem((2, 2, *panel), BF16),
            vmem((2, 2, *panel), BF16),
            vmem((5, *panel), BF16),
            vmem((5, *panel), BF16),
            vmem(panel, BF16),
            dma((16,)), dma((9,)), dma((5, 2)), dma((5, 2)), dma((2, 3)), dma((2, 3)), dma((RING,)), dma((RING,)),
            dma((SIDE,)), dma((SIDE,)), dma((SIDE,)), dma((SIDE,)),
            dma((2, SIDE)), dma((2, SIDE)), dma((SIDE,)), dma((SIDE,)),
            dma((SIDE,)), dma((SIDE,)), dma((SIDE,)), dma((SIDE,)),
            dma((RING,)), dma((RING,)), dma((8,)), dma((8,)), dma((RING,)), dma((RING,)),
            dma((RING,)), dma((RING,)), dma((2, 3)), dma((2, 3)), dma((5, 2)), dma((5, 2)), dma((2,)), dma((2,)),
        ],
        compiler_params=pltpu.CompilerParams(
            collective_id=0, has_side_effects=True, vmem_limit_bytes=VMEM_BYTES
        ),
    )(
        features_t, tile_values, jnp.transpose(tile_rows, (2, 0, 1)), jnp.transpose(tile_cols, (2, 0, 1)),
        tile_count, weight, cotangent_t,
    )
    return pl.pallas_call(
        hand_over,
        out_shape=out_shape,
        in_specs=[pl.BlockSpec(memory_space=vmem)] * 4,
        out_specs=(pl.BlockSpec(memory_space=vmem),) * 3,
    )(*results)


def solution(mesh):
    return jax.shard_map(
        body,
        mesh=mesh,
        in_specs=(
            P("feat", "blk"),
            P("blk", None, None, None, None),
            P("blk", None, None),
            P("blk", None, None),
            P("blk", None),
            P("feat", None),
            P("feat", "blk"),
        ),
        out_specs=(P("feat", "blk"), P("feat", None), P("feat", "blk")),
        check_vma=False,
    )
```

```python
import jax
import jax.numpy as jnp
from jax import lax
from jax.experimental import pallas as pl
from jax.experimental.pallas import tpu as pltpu
from jax.sharding import PartitionSpec as P

MESH = pl.DeviceIdType.MESH
BF16, F32 = jnp.bfloat16, jnp.float32
RING = 8
SIDE = 4
SLOTS = 12
TILE = 128
ROWS = 64
NODES = 512
PARTS = 32
HALF = ROWS // 2
VMEM_BYTES = 62 * 1024 * 1024

ORDER = [(d, cc) for d in (0, 1, 7, 2, 6, 3, 5, 4) for cc in (0, 1)]
PLACE = {pair: n for n, pair in enumerate(ORDER)}
DIRECT = {2: 0, 6: 1, 1: 2, 7: 3, 0: 4}


def kernel(
    feat, tiles, rows_hbm, cols_hbm, count_hbm, weight, cot,
    hid, wgrad, fin_own, fin_other,
    tile_rows, tile_cols, tile_count,
    raw, acc, dense, panels, agg, w_all, w_turned, cot_all,
    agg_out, agg_in, hid_out, sig_out, sig_in,
    g1_out, g1, g2_out, g2, g3_out, g3, g4_out,
    back_out, back_in, keep, near_out, near_in, root_out, root_in, fin_out,
    tile_sem, local_sem, first_send, first_recv, second_send, second_recv, core_send, core_recv,
    w_send, w_recv, cot_send, cot_recv, agg_send, agg_recv, sig_send, sig_recv,
    hid_send, hid_recv, g1_send, g1_recv, g2_send, g2_recv, g3_send, g3_recv, g4_send, g4_recv,
    back_send, back_recv, near_send, near_recv, root_send, root_recv, fin_send, fin_recv,
):
    p, r, f = lax.axis_index("blk"), lax.axis_index("rep"), lax.axis_index("feat")
    z, xh, c = p // 4, (p // 2) % 2, p % 2
    lane = (c + r) % 2

    def at(dz=0, dx=0, dc=0, dr=0, df=0):
        nz = (z + dz) % RING
        nx, nc, nr = (xh + dx) % 2, (c + dc) % 2, (r + dr) % 2
        return (nz * 4 + nx * 2 + nc, nr, (f + df) % SIDE)

    pending = []

    def go(copy):
        copy.start()
        pending.append(copy)

    def remote(src, dst, send, recv, device):
        return pltpu.make_async_remote_copy(
            src_ref=src, dst_ref=dst, send_sem=send, recv_sem=recv, device_id=device, device_id_type=MESH
        )

    partners = [at(dz=dz) for dz in (4, 3, 5, 2, 6, 1, 7)]
    partners += [at(dz=dz, dx=1, dc=1, dr=1) for dz in (2, 6, 1, 7, 0)]
    partners += [at(dr=dr, df=df) for df in (2, 1, 3, 0) for dr in range(2) if dr or df]
    partners += [at(dc=1), at(dx=1), at(dx=1, dr=1), at(dc=1, dr=1), at(dx=1, dc=1)]
    barrier = pltpu.get_barrier_semaphore()
    for device in partners:
        pl.semaphore_signal(barrier, inc=1, device_id=device, device_id_type=MESH)

    def tile_copy(n):
        half = n // 2
        odd, step = half % 2, (half + 1) // 2
        d = (odd * step + (1 - odd) * (RING - step)) % RING
        source = ((z + RING - d) % RING) * 4 + ((xh + lane + n % 2) % 2) * 2 + r
        section = (p + PARTS - source) % PARTS
        return section, pltpu.make_async_copy(tiles.at[0, section], raw.at[n], tile_sem.at[n])

    own_feat = pltpu.make_async_copy(feat, panels.at[0, 0], local_sem.at[0])
    own_w = pltpu.make_async_copy(weight, w_all.at[f], local_sem.at[1])
    own_lanes = pl.ds(pl.multiple_of(f * TILE, TILE), TILE)
    own_cot = pltpu.make_async_copy(cot.at[:, own_lanes], cot_all.at[f], local_sem.at[2])

    scalar_copies = [
        pltpu.make_async_copy(src, dst, local_sem.at[3 + i])
        for i, (src, dst) in enumerate(((rows_hbm, tile_rows), (cols_hbm, tile_cols), (count_hbm, tile_count)))
    ]
    for copy in scalar_copies:
        copy.start()

    @pl.when(lane == 0)
    def _():
        own_feat.start()

    own_w.start()
    own_cot.start()

    def start_tiles(n, carried):
        tile_copy(n)[1].start()
        return carried

    lax.fori_loop(0, 16, start_tiles, 0)

    acc[SLOTS] = jnp.zeros((TILE, TILE), BF16)
    agg[...] = jnp.zeros_like(agg)
    pl.semaphore_wait(barrier, len(partners))

    def home(dz):
        return at(dz=dz, dx=lane, dc=lane, dr=lane)

    def first_copy(d, chunk):
        span = pl.ds(chunk * HALF, HALF) if d in (2, 6) else pl.ds(0, ROWS)
        return remote(
            feat.at[span], panels.at[d, 0, span],
            first_send.at[DIRECT[d], chunk], first_recv.at[DIRECT[d], chunk], home(d),
        )

    for i in range(2):
        for d in (2, 6):
            go(first_copy(d, i ^ (d == 6)))
    for d in (1, 7):
        go(first_copy(d, 0))

    @pl.when(lane == 1)
    def _():
        first_copy(0, 0).start()

    def second_copy(way, part):
        d = 2 if way == 0 else RING - 2
        step = 2 if part == 2 else 1
        to = d + step if way == 0 else d - step
        chunk = part if part < 2 else way
        span = pl.ds(chunk * HALF, HALF)
        return remote(
            panels.at[d, 0, span], panels.at[to, 0, span],
            second_send.at[way, part], second_recv.at[way, part], at(dz=step if way == 0 else RING - step),
        )

    def core_copy(d):
        return remote(panels.at[d, 0], panels.at[d, 1], core_send.at[d], core_recv.at[d], at(dc=1))

    def w_copy(df):
        return remote(weight, w_all.at[f], w_send.at[df], w_recv.at[df], at(df=df))

    def cot_copy(df):
        lanes = pl.ds(pl.multiple_of(((f + df) % SIDE) * TILE, TILE), TILE)
        return remote(cot.at[:, lanes], cot_all.at[f], cot_send.at[df], cot_recv.at[df], at(df=df))

    for df in range(1, SIDE):
        go(w_copy(df))
        go(cot_copy(df))

    def densify(n, carried):
        section, copy = tile_copy(n)
        copy.wait()
        live = tile_count[0, section]
        target = [
            jnp.where(t < live, tile_rows[t, 0, section] * SIDE + tile_cols[t, 0, section], 16)
            for t in range(SLOTS)
        ]
        for t in range(SLOTS):
            before = jnp.int32(SLOTS)
            for u in range(t):
                before = jnp.where(target[u] == target[t], u, before)
            acc[t] = raw[n, t] + acc[before]
        for b in range(16):
            last = jnp.int32(SLOTS)
            for t in range(SLOTS):
                last = jnp.where(target[t] == b, t, last)
            i, j = b // SIDE, b % SIDE
            dense[n, i * TILE:(i + 1) * TILE, j * TILE:(j + 1) * TILE] = acc[last]
        return carried

    def forward(d, cc):
        if cc:
            core_copy(d).wait_recv()
        agg[...] += lax.dot_general(
            panels[d, cc], dense[PLACE[d, cc]], (((1,), (1,)), ((), ())), preferred_element_type=F32
        )

    for copy in scalar_copies:
        copy.wait()
    lax.fori_loop(0, 16, densify, 0)
    for i in range(2):
        for way in range(2):
            chunk = i ^ way
            first_copy(2 if way == 0 else 6, chunk).wait_recv()
            if i == 0:
                go(second_copy(way, 2))
            go(second_copy(way, chunk))
    go(core_copy(2))
    go(core_copy(6))
    for d in (1, 7):
        first_copy(d, 0).wait_recv()
        go(core_copy(d))

    @pl.when(lane == 0)
    def _():
        own_feat.wait()

    @pl.when(lane == 1)
    def _():
        first_copy(0, 0).wait_recv()

    go(core_copy(0))
    for d in (2, 6, 1, 7, 0):
        forward(d, 0)
        forward(d, 1)
    own_w.wait()
    for df in range(1, SIDE):
        w_copy(df).wait_recv()
    w_turned[...] = w_all[...].reshape(256, 256).astype(F32).T.astype(BF16)
    for way in range(2):
        second_copy(way, 0).wait_recv()
        second_copy(way, 1).wait_recv()
        go(core_copy(3 if way == 0 else 5))
    forward(3, 0)
    for way in range(2):
        second_copy(way, 2).wait_recv()
    go(core_copy(4))
    forward(5, 0)
    forward(4, 0)
    for d in (3, 5, 4):
        forward(d, 1)

    def agg_copy(dr, df):
        return remote(
            agg_out.at[(f + df) % SIDE], agg_in.at[r, f], agg_send.at[dr, df], agg_recv.at[dr, df], at(dr=dr, df=df)
        )

    group = [(dr, df) for df in (2, 1, 3, 0) for dr in (1, 0) if dr or df]
    for b in range(SIDE):
        agg_out[b] = agg[:, b * TILE:(b + 1) * TILE].astype(BF16)
    for dr, df in group:
        go(agg_copy(dr, df))
    agg_in[r, f] = agg_out[f]
    own_cot.wait()
    for df in range(1, SIDE):
        cot_copy(df).wait_recv()
    for dr, df in group:
        agg_copy(dr, df).wait_recv()
    summed = (agg_in[0].astype(F32) + agg_in[1].astype(F32)).reshape(256, TILE).astype(BF16)
    pre_act = jnp.dot(w_turned[...], summed, preferred_element_type=F32)
    gate = 1.0 / (1.0 + jnp.exp(-pre_act))
    grad = cot_all[...].reshape(256, TILE).astype(F32)
    pre_grad = (grad * gate * (1.0 + pre_act * (1.0 - gate))).astype(BF16)
    signal = jnp.dot(w_all[...].reshape(256, 256), pre_grad, preferred_element_type=F32)
    sig_out[...] = signal.astype(BF16).reshape(SIDE, ROWS, TILE)

    def sig_copy(df):
        return remote(sig_out.at[(f + df) % SIDE], sig_in.at[f], sig_send.at[df], sig_recv.at[df], at(df=df))

    for df in (2, 1, 3):
        go(sig_copy(df))
    sig_in[f] = sig_out[f]

    grad_rows = jnp.where(r == 0, pre_grad[:TILE].astype(F32), pre_grad[TILE:].astype(F32)).astype(BF16)
    share = lax.dot_general(summed, grad_rows, (((1,), (1,)), ((), ())), preferred_element_type=F32)
    g1_out[...] = share.astype(BF16).reshape(SIDE, ROWS, TILE)

    def g1_copy(df):
        return remote(g1_out.at[(f + df) % SIDE], g1.at[f], g1_send.at[df], g1_recv.at[df], at(df=df))

    for df in range(1, SIDE):
        go(g1_copy(df))
    g1[f] = g1_out[f]

    hid_out[...] = (pre_act * gate).astype(BF16).reshape(SIDE, ROWS, TILE)

    def hid_copy(df):
        return remote(
            hid_out.at[(f + df) % SIDE], hid.at[:, own_lanes], hid_send.at[df], hid_recv.at[df], at(df=df)
        )

    own_hid = pltpu.make_async_copy(hid_out.at[f], hid.at[:, own_lanes], local_sem.at[6])
    own_hid.start()
    for df in range(1, SIDE):
        go(hid_copy(df))

    for df in (2, 1, 3):
        sig_copy(df).wait_recv()
    signal_row = jnp.concatenate([sig_in[b] for b in range(SIDE)], axis=1)

    def backward(d, cc):
        return jnp.dot(signal_row, dense[PLACE[d, cc]], preferred_element_type=F32)

    def back_copy(d):
        return remote(back_out.at[d], back_in.at[d], back_send.at[d], back_recv.at[d], at(dc=1))

    def give(d):
        back_out[d] = backward(d, 1).astype(BF16)
        go(back_copy(d))

    def take(d):
        keep[d] = backward(d, 0)
        back_copy(d).wait_recv()
        keep[d] += back_in[d].astype(F32)

    def near_copy(way, part):
        d = 4 if part == 2 else (3 if way == 0 else 5)
        step = 2 if part == 2 else 1
        span = pl.ds((part if part < 2 else way) * HALF, HALF)
        return remote(
            near_out.at[way, step - 1, span], near_in.at[way, step - 1, span],
            near_send.at[way, part], near_recv.at[way, part], at(dz=RING - step if way == 0 else step),
        )

    def root_copy(d, chunk):
        span = pl.ds(chunk * HALF, HALF) if d in (2, 6) else pl.ds(0, ROWS)
        return remote(
            root_out.at[DIRECT[d], span], root_in.at[DIRECT[d], span],
            root_send.at[DIRECT[d], chunk], root_recv.at[DIRECT[d], chunk], home(RING - d),
        )

    halves = [slice(0, HALF), slice(HALF, ROWS)]
    for d in (4, 3, 5):
        give(d)
    take(4)
    for way in range(2):
        near_out[way, 1, halves[way]] = keep[4, halves[way]].astype(BF16)
        go(near_copy(way, 2))
    for df in range(1, SIDE):
        g1_copy(df).wait_recv()
    g2_out[...] = jnp.sum(g1[...].astype(F32), axis=0)

    def g2_copy(dz):
        rows = pl.ds(pl.multiple_of(((z + dz) % RING) * 8, 8), 8)
        return remote(g2_out.at[rows], g2.at[z], g2_send.at[dz], g2_recv.at[dz], at(dz=dz))

    for dz in range(1, RING):
        go(g2_copy(dz))
    g2[z] = g2_out[pl.ds(pl.multiple_of(z * 8, 8), 8)]

    for way in range(2):
        take(3 if way == 0 else 5)
        near_out[way, 0] = keep[3 if way == 0 else 5].astype(BF16)
        go(near_copy(way, way))
        go(near_copy(way, 1 - way))
    for d in (2, 6, 1, 7, 0):
        give(d)
    take(2)
    take(6)
    for d in (1, 7):
        take(d)
        root_out[DIRECT[d]] = keep[d].astype(BF16)
        go(root_copy(d, 0))

    take(0)

    @pl.when(lane == 1)
    def _():
        root_out[DIRECT[0]] = keep[0].astype(BF16)
        root_copy(0, 0).start()


    for dz in range(1, RING):
        g2_copy(dz).wait_recv()
    g3_out[...] = jnp.sum(g2[...], axis=0)

    def g3_copy(i):
        return remote(
            g3_out, g3.at[r * 4 + xh * 2 + c], g3_send.at[i], g3_recv.at[i],
            at(dx=i // 4, dc=(i // 2) % 2, dr=i % 2),
        )

    for i in range(1, 8):
        go(g3_copy(i))
    g3[r * 4 + xh * 2 + c] = g3_out[...]

    for i in range(2):
        for way in range(2):
            chunk, d = i ^ way, 2 if way == 0 else 6
            value = keep[d, halves[chunk]]
            near_copy(way, chunk).wait_recv()
            value = value + near_in[way, 0, halves[chunk]].astype(F32)
            if i == 0:
                near_copy(way, 2).wait_recv()
                value = value + near_in[way, 1, halves[chunk]].astype(F32)
            root_out[DIRECT[d], halves[chunk]] = value.astype(BF16)
            go(root_copy(d, chunk))

    for i in range(1, 8):
        g3_copy(i).wait_recv()
    scale = float(NODES * PARTS) ** -0.5
    for half in range(2):
        four = (g3[4 * half] + g3[4 * half + 1]) + (g3[4 * half + 2] + g3[4 * half + 3])
        g4_out[:, half * TILE:(half + 1) * TILE] = four * scale
    own_rows = pl.ds(pl.multiple_of(z * 8, 8), 8)

    def g4_copy(dz):
        return remote(g4_out, wgrad.at[own_rows], g4_send.at[dz], g4_recv.at[dz], at(dz=dz))

    for dz in range(1, RING):
        go(g4_copy(dz))
    own_wgrad = pltpu.make_async_copy(g4_out, wgrad.at[own_rows], local_sem.at[7])
    own_wgrad.start()

    def fin_copy(chunk):
        span = pl.ds(chunk * HALF, HALF)
        return remote(fin_out.at[span], fin_other.at[span], fin_send.at[chunk], fin_recv.at[chunk], at(dr=1))

    @pl.when(lane == 0)
    def _():
        root_in[DIRECT[0]] = keep[0].astype(BF16)

    @pl.when(lane == 1)
    def _():
        root_copy(0, 0).wait_recv()

    for d in (1, 7):
        root_copy(d, 0).wait_recv()
    for chunk in range(2):
        value = root_in[DIRECT[0], halves[chunk]].astype(F32)
        for d in (1, 7, 2, 6):
            if d in (2, 6):
                root_copy(d, chunk).wait_recv()
            value = value + root_in[DIRECT[d], halves[chunk]].astype(F32)
        fin_out[halves[chunk]] = value.astype(BF16)
        go(fin_copy(chunk))
    own_fin = pltpu.make_async_copy(fin_out, fin_own, local_sem.at[8])
    own_fin.start()

    for chunk in range(2):
        fin_copy(chunk).wait_recv()

    @pl.when(lane == 1)
    def _():
        first_copy(0, 0).wait_send()
        root_copy(0, 0).wait_send()

    for copy in pending:
        copy.wait_send()
    for df in range(1, SIDE):
        hid_copy(df).wait_recv()
    for dz in range(1, RING):
        g4_copy(dz).wait_recv()
    own_hid.wait()
    own_wgrad.wait()
    own_fin.wait()


def hand_over(hid, wgrad, fin_own, fin_other, hid_to, wgrad_to, igrad_to):
    hid_to[...] = hid[...]
    wgrad_to[...] = wgrad[...]
    igrad_to[...] = (fin_own[...].astype(F32) + fin_other[...].astype(F32)).astype(BF16)


def body(features_t, tile_values, tile_rows, tile_cols, tile_count, weight, cotangent_t):
    anywhere = pl.BlockSpec(memory_space=pl.ANY)
    vmem, dma = pltpu.VMEM, pltpu.SemaphoreType.DMA
    block = (SIDE, ROWS, TILE)
    panel = (ROWS, NODES)
    out_shape = (
        jax.ShapeDtypeStruct((ROWS, NODES), BF16),
        jax.ShapeDtypeStruct((ROWS, 256), F32),
        jax.ShapeDtypeStruct((ROWS, NODES), BF16),
    )
    results = pl.pallas_call(
        kernel,
        out_shape=(*out_shape, out_shape[2]),
        in_specs=[anywhere] * 7,
        out_specs=(anywhere,) * 4,
        scratch_shapes=[
            pltpu.SMEM((SLOTS, 1, PARTS), jnp.int32),
            pltpu.SMEM((SLOTS, 1, PARTS), jnp.int32),
            pltpu.SMEM((1, PARTS), jnp.int32),
            vmem((16, SLOTS, TILE, TILE), BF16),
            vmem((SLOTS + 1, TILE, TILE), BF16),
            vmem((16, NODES, NODES), BF16),
            vmem((RING, 2, *panel), BF16),
            vmem(panel, F32),
            vmem((SIDE, ROWS, 256), BF16),
            vmem((256, 256), BF16),
            vmem(block, BF16),
            vmem(block, BF16),
            vmem((2, *block), BF16),
            vmem(block, BF16),
            vmem(block, BF16),
            vmem(block, BF16),
            vmem(block, BF16),
            vmem(block, BF16),
            vmem((ROWS, TILE), F32),
            vmem((RING, 8, TILE), F32),
            vmem((8, TILE), F32),
            vmem((8, 8, TILE), F32),
            vmem((8, 256), F32),
            vmem((RING, *panel), BF16),
            vmem((RING, *panel), BF16),
            vmem((RING, *panel), F32),
            vmem((2, 2, *panel), BF16),
            vmem((2, 2, *panel), BF16),
            vmem((5, *panel), BF16),
            vmem((5, *panel), BF16),
            vmem(panel, BF16),
            dma((16,)), dma((9,)), dma((5, 2)), dma((5, 2)), dma((2, 3)), dma((2, 3)), dma((RING,)), dma((RING,)),
            dma((SIDE,)), dma((SIDE,)), dma((SIDE,)), dma((SIDE,)),
            dma((2, SIDE)), dma((2, SIDE)), dma((SIDE,)), dma((SIDE,)),
            dma((SIDE,)), dma((SIDE,)), dma((SIDE,)), dma((SIDE,)),
            dma((RING,)), dma((RING,)), dma((8,)), dma((8,)), dma((RING,)), dma((RING,)),
            dma((RING,)), dma((RING,)), dma((2, 3)), dma((2, 3)), dma((5, 2)), dma((5, 2)), dma((2,)), dma((2,)),
        ],
        compiler_params=pltpu.CompilerParams(
            collective_id=0, has_side_effects=True, vmem_limit_bytes=VMEM_BYTES
        ),
    )(
        features_t, tile_values, jnp.transpose(tile_rows, (2, 0, 1)), jnp.transpose(tile_cols, (2, 0, 1)),
        tile_count, weight, cotangent_t,
    )
    return pl.pallas_call(
        hand_over,
        out_shape=out_shape,
        in_specs=[pl.BlockSpec(memory_space=vmem)] * 4,
        out_specs=(pl.BlockSpec(memory_space=vmem),) * 3,
    )(*results)


def solution(mesh):
    return jax.shard_map(
        body,
        mesh=mesh,
        in_specs=(
            P("feat", "blk"),
            P("blk", None, None, None, None),
            P("blk", None, None),
            P("blk", None, None),
            P("blk", None),
            P("feat", None),
            P("feat", "blk"),
        ),
        out_specs=(P("feat", "blk"), P("feat", None), P("feat", "blk")),
        check_vma=False,
    )
```
